256 devices in a mesh: grp: 4 (over z_lo), seq: 64 (over x, z_hi, y, core).
Axes of the slice: x: 4, y: 4, z: 8 (z_hi: 2, z_lo: 4; z = z_hi * 4 + z_lo), core: 2. Of those that a mesh axis runs over, the one named last changes fastest.
Arguments:
- queries: bfloat16 [65536, 2560], P(('grp', 'seq')), may hold values from -150 to 150, as said below
- key_matrix: bfloat16 [65536, 2560], P(('grp', 'seq')), may hold values from -4 to 4, as said below
- value_matrix: bfloat16 [65536, 2560], P(('grp', 'seq')), may hold values from -6 to 6
Outputs:
- attended: bfloat16 [65536, 2560], P(('grp', 'seq'))
The draws below stay inside these ranges and needn't reach their ends.
Inputs may be any that keep to these rules, and one draw needn't show every extreme that they name: `key_matrix`: keys are of order one. `queries`: queries are of order one in the shown draw.
All inputs are finite; a program needn't handle non-finite values.
Results may differ from the reference program's by a relative error of at most 0.001.
The reference program's roundings to bfloat16 on the way (of `rounded`) count: a program that leaves them out, or rounds other values in their place, can miss the bound.
Values may be sent and summed in bfloat16 or wider, within the bound.
A program may use at most 128 MiB of HBM per device.

```python
import jax
import jax.numpy as jnp
from jax import lax

ATTENTION_HEADS = 32
HEAD = 80
LOCAL_LENGTH = 256
COARSE_DILATION = 16
WHOLE_DILATION = 128
COARSE_LENGTH = 16384
SEQUENCE_LENGTH = 65536


def key_base(key):
    return jnp.clip(jax.random.normal(key, (SEQUENCE_LENGTH, ATTENTION_HEADS * HEAD), jnp.float32), -4.0, 4.0)


def draw_queries(key, part):
    key = jax.random.fold_in(key, 11)
    own = jnp.clip(jax.random.normal(key, (SEQUENCE_LENGTH, ATTENTION_HEADS * HEAD), jnp.float32), -4.0, 4.0)
    return own.astype(jnp.bfloat16)


def draw_key_matrix(key, part):
    base = key_base(key)
    return base.astype(jnp.bfloat16)


def levels(key, shape, cuts, low, top_value):
    loudness, own = 1.0, jax.random.fold_in(key, 6)
    for axis_at, shards_of in cuts:
        heights = jnp.exp(jax.random.uniform(jax.random.fold_in(own, axis_at), (shards_of,), jnp.float32, low / len(cuts), top_value / len(cuts)))
        loudness = loudness * jnp.repeat(heights, shape[axis_at] // shards_of).reshape([-1 if axis == axis_at else 1 for axis in range(len(shape))])
    return loudness


def normal_values(rng, dims, width, most, cuts=(), dtype=jnp.bfloat16):
    array = jax.random.normal(rng, dims, jnp.float32) * width
    if len(cuts) > 0:
        array = levels(rng, dims, cuts, -0.22, 0.18) * array
    return jnp.clip(array, min=-most, max=most).astype(dtype)


def setup_inputs(seed: int = 0) -> dict:
    seeds = jax.random.split(jax.random.key(seed), 4)
    return {
        "queries": draw_queries(jax.random.fold_in(seeds[3], 71), 0),
        "key_matrix": draw_key_matrix(jax.random.fold_in(seeds[3], 71), 0),
        "value_matrix": normal_values(seeds[2], (SEQUENCE_LENGTH, ATTENTION_HEADS * HEAD), 1.0, 6.0, ((0, 256),)),
    }


lowest_score = -1e30


def dilated_attend(field, stride, count_of_heads):
    total_rows = field.shape[0]
    head_width = field.shape[1] // count_of_heads
    reshaped_rows = field.reshape(total_rows // stride, stride, count_of_heads, head_width)
    return reshaped_rows[:, jnp.arange(count_of_heads) % stride, jnp.arange(count_of_heads), :]


def attend(items):
    query_part, key_part, value_part = items
    head_width = query_part.shape[2]
    count = query_part.shape[0]
    scores = jnp.einsum("qhe,khe->hqk", query_part.astype(jnp.float32), key_part.astype(jnp.float32)) * (head_width ** -0.5)
    allowed = jnp.arange(count)[:, None] >= jnp.arange(count)[None, :]
    scores = jnp.where(allowed[None], scores, lowest_score)
    row_top = jnp.max(scores, axis=2)
    weights = jnp.where(allowed[None], jnp.exp(scores - row_top[:, :, None]), 0.0)
    row_mass = jnp.sum(weights, axis=2)
    rounded = lax.optimization_barrier(weights.astype(jnp.bfloat16)).astype(jnp.float32)
    weighted = jnp.einsum("hqk,khe->hqe", rounded, value_part.astype(jnp.float32))
    return weighted / row_mass[:, :, None], row_top + jnp.log(row_mass)


def level_attend(queries, key_matrix, value_matrix, stride, segment, count_of_heads):
    rows_seg = segment // stride
    pieces = []
    for field in (queries, key_matrix, value_matrix):
        picked = dilated_attend(field, stride, count_of_heads)
        pieces.append(picked.reshape(picked.shape[0] // rows_seg, rows_seg, count_of_heads, picked.shape[2]))
    return lax.map(attend, tuple(pieces))


def merge_levels(local_level, coarse_level_result, whole_level_result, mid_stride, far_stride):
    out_one, lse_one = local_level
    count_of_heads = out_one.shape[0]
    head_width = out_one.shape[2]

    def spread(state, stride):
        out_part, lse_part = state
        count = out_part.shape[1]
        chosen = jnp.arange(stride)[None, :] == (jnp.arange(count_of_heads) % stride)[:, None]
        lse_wide = jnp.where(chosen[:, None, :], lse_part[:, :, None], lowest_score).reshape(count_of_heads, count * stride)
        out_wide = jnp.broadcast_to(out_part[:, :, None, :], (count_of_heads, count, stride, head_width)).reshape(count_of_heads, count * stride, head_width)
        return out_wide, lse_wide

    out_two, lse_two = spread(coarse_level_result, mid_stride)
    out_three, lse_three = spread(whole_level_result, far_stride)
    best = jnp.maximum(lse_one, jnp.maximum(lse_two, lse_three))
    factor_one = jnp.exp(lse_one - best)
    factor_two = jnp.exp(lse_two - best)
    factor_three = jnp.exp(lse_three - best)
    combined = factor_one[:, :, None] * out_one + factor_two[:, :, None] * out_two + factor_three[:, :, None] * out_three
    combined = combined / (factor_one + factor_two + factor_three)[:, :, None]
    return combined.transpose(1, 0, 2).reshape(-1, count_of_heads * head_width).astype(jnp.bfloat16)


def regroup_rows(out_part, lse_part, segment_count, per_segment):
    count_of_heads = out_part.shape[1]
    head_width = out_part.shape[3]
    flat_out = out_part.transpose(1, 0, 2, 3).reshape(count_of_heads, segment_count, per_segment, head_width).transpose(1, 0, 2, 3)
    flat_lse = lse_part.transpose(1, 0, 2).reshape(count_of_heads, segment_count, per_segment).transpose(1, 0, 2)
    return flat_out, flat_lse


def reference(queries, key_matrix, value_matrix):
    segment_count = SEQUENCE_LENGTH // LOCAL_LENGTH
    coarse_output, coarse_logsumexp = level_attend(queries, key_matrix, value_matrix, COARSE_DILATION, COARSE_LENGTH, ATTENTION_HEADS)
    whole_output, whole_logsumexp = level_attend(queries, key_matrix, value_matrix, WHOLE_DILATION, SEQUENCE_LENGTH, ATTENTION_HEADS)
    coarse_output, coarse_logsumexp = regroup_rows(coarse_output, coarse_logsumexp, segment_count, LOCAL_LENGTH // COARSE_DILATION)
    whole_output, whole_logsumexp = regroup_rows(whole_output, whole_logsumexp, segment_count, LOCAL_LENGTH // WHOLE_DILATION)

    def one(items):
        query_part, key_part, value_part, coarse_partial, coarse_level, whole_partial, whole_level = items
        local_level = attend((query_part.reshape(LOCAL_LENGTH, ATTENTION_HEADS, HEAD), key_part.reshape(LOCAL_LENGTH, ATTENTION_HEADS, HEAD), value_part.reshape(LOCAL_LENGTH, ATTENTION_HEADS, HEAD)))
        return merge_levels(local_level, (coarse_partial, coarse_level), (whole_partial, whole_level), COARSE_DILATION, WHOLE_DILATION)

    blocks = lax.map(one, (queries.reshape(segment_count, LOCAL_LENGTH, ATTENTION_HEADS * HEAD), key_matrix.reshape(segment_count, LOCAL_LENGTH, ATTENTION_HEADS * HEAD), value_matrix.reshape(segment_count, LOCAL_LENGTH, ATTENTION_HEADS * HEAD), coarse_output, coarse_logsumexp, whole_output, whole_logsumexp))
    return blocks.reshape(SEQUENCE_LENGTH, ATTENTION_HEADS * HEAD)
```

```python
import functools

import jax
import jax.numpy as jnp
from jax import lax
from jax.experimental import pallas as pl
from jax.experimental.pallas import tpu as pltpu
from jax.sharding import PartitionSpec as P

HEADS = 32
HEAD = 80
WIDTH = HEADS * HEAD
ROWS = 256
COARSE = 16
WHOLE = 128
LANES = 128
GROUP = 8
SPAN = GROUP * HEAD
GROUPS = HEADS // GROUP
SEQ = 64
GRP = 4
PICKS = ROWS // COARSE
COARSE_ROWS = SEQ * PICKS
FAR = ROWS // WHOLE * SEQ
SCALE = HEAD**-0.5
LOG2E = 1.4426950408889634
LOWEST = -1e30
MESH = pl.DeviceIdType.MESH
F32, BF16 = jnp.float32, jnp.bfloat16

NT = (((1,), (1,)), ((), ()))
NN = (((1,), (0,)), ((), ()))


def dot(a, b, dims=NN):
    return lax.dot_general(a, b, dims, preferred_element_type=F32)


def iota(shape, axis):
    return lax.broadcasted_iota(jnp.int32, shape, axis)


def head_of(lane):
    return (lane * 52429) >> 22


def eye(n):
    return jnp.where(iota((n, n), 0) == iota((n, n), 1), 1.0, 0.0).astype(BF16)


def window(hh):
    tile, shift = HEAD * hh // LANES, HEAD * hh % LANES
    return tile, shift, 1 if shift + HEAD <= LANES else 2


def in_circle(lane, start, length):
    return ((lane - start) & (LANES - 1)) < length


def group_mask(group):
    shape = (COARSE, SPAN)
    residue = (head_of(iota(shape, 1)) + group * GROUP) & (COARSE - 1)
    return jnp.where(iota(shape, 0) == residue, 1.0, 0.0).astype(BF16)


def pick(x, mask, gather):
    masked = (x.reshape(PICKS, COARSE, SPAN) * mask[None]).reshape(ROWS, SPAN)
    return dot(gather, masked)


def pack_group(group, q, k, v, mask, gather, send, q_pick):
    lane = iota((PICKS, LANES), 1)
    qp, kp, vp = (pick(x, mask, gather) for x in (q, k, v))
    q_pick[group] = qp.astype(BF16)
    for hh in range(GROUP):
        tile, shift, tiles = window(hh)

        def circle(x):
            first = x[:, LANES * tile : LANES * (tile + 1)]
            if tiles == 1:
                return first
            return jnp.where(lane >= shift, first, x[:, LANES * (tile + 1) : LANES * (tile + 2)])

        own = in_circle(lane, shift, HEAD)
        vc = circle(vp)
        head = group * GROUP + hh
        send[head, :, :LANES] = jnp.where(own, circle(kp), pltpu.roll(vc, HEAD, 1)).astype(BF16)
        send[head, :, LANES:] = jnp.where(own, circle(qp), pltpu.roll(vc, 32, 1)).astype(BF16)


def local_group(group, q, k, v, out_t):
    unit = eye(LANES)
    half = ROWS // 2
    v_t = jnp.concatenate(
        [dot(unit, v[:, LANES * j : LANES * (j + 1)], NT).astype(BF16) for j in range(SPAN // LANES)], axis=0
    )
    allowed = iota((half, half), 0) <= iota((half, half), 1)
    for hh in range(GROUP):
        tile, shift, tiles = window(hh)
        cols = slice(LANES * tile, LANES * (tile + tiles))
        lane = iota((1, LANES * tiles), 1)
        own = jnp.where((lane >= shift) & (lane < shift + HEAD), 1.0, 0.0).astype(BF16)
        s = dot(k[:, cols], q[:, cols] * own, NT)
        s00 = jnp.where(allowed, s[:half, :half], LOWEST)
        s01 = s[:half, half:]
        s11 = jnp.where(allowed, s[half:, half:], LOWEST)
        top0 = jnp.max(s00, axis=0, keepdims=True)
        top1 = jnp.maximum(jnp.max(s01, axis=0, keepdims=True), jnp.max(s11, axis=0, keepdims=True))
        w00 = jnp.exp2((s00 - top0) * (SCALE * LOG2E))
        w01 = jnp.exp2((s01 - top1) * (SCALE * LOG2E))
        w11 = jnp.exp2((s11 - top1) * (SCALE * LOG2E))
        mass0 = jnp.sum(w00, axis=0, keepdims=True)
        mass1 = jnp.sum(w01, axis=0, keepdims=True) + jnp.sum(w11, axis=0, keepdims=True)
        w = jnp.concatenate(
            [
                jnp.concatenate([w00.astype(BF16), w01.astype(BF16)], axis=1),
                jnp.concatenate([jnp.zeros((half, half), BF16), w11.astype(BF16)], axis=1),
            ],
            axis=0,
        )
        o = dot(v_t[HEAD * hh : HEAD * (hh + 1)], w)
        o = o * (1.0 / jnp.concatenate([mass0, mass1], axis=1))
        out_t[pl.ds(pl.multiple_of(group * SPAN + HEAD * hh, 16), HEAD), :] = o.astype(BF16)


def local_picks(group, q_pick, k, v, o_pick, lse_pick):
    shape = (GROUP * PICKS, SPAN)
    own = (iota(shape, 0) >> 4) == head_of(iota(shape, 1))
    q = jnp.concatenate([q_pick] * GROUP, axis=0) * jnp.where(own, 1.0, 0.0).astype(BF16)
    s = dot(q, k, NT)
    row, key = iota(s.shape, 0), iota(s.shape, 1)
    residue = ((row >> 4) + group * GROUP) & (COARSE - 1)
    s = jnp.where(key <= (row & (PICKS - 1)) * COARSE + residue, s, LOWEST)
    top = jnp.max(s, axis=1, keepdims=True)
    w = jnp.exp2((s - top) * (SCALE * LOG2E))
    mass = jnp.sum(w, axis=1, keepdims=True)
    o = dot(w.astype(BF16), v) * (1.0 / mass)
    lse = top * SCALE + jnp.log(mass)
    cols = pl.ds(pl.multiple_of(group * SPAN, LANES), SPAN)
    o_pick[:, cols] = jnp.sum(jnp.where(own, o, 0.0).reshape(GROUP, PICKS, SPAN), axis=0)
    lse_pick[:, cols] = jnp.sum(jnp.where(own, lse, 0.0).reshape(GROUP, PICKS, SPAN), axis=0)


def attend(q, keys, allowed, lane, turn):
    s = dot(q, keys[:, :LANES], NT)
    s = allowed(s)
    top = jnp.max(s, axis=1, keepdims=True)
    w = jnp.exp2((s - top) * (SCALE * LOG2E))
    mass = jnp.sum(w, axis=1, keepdims=True)
    both = dot(w.astype(BF16), keys)
    o = jnp.where(in_circle(lane, turn + HEAD, 48), both[:, :LANES], pltpu.roll(both[:, LANES:], 48, 1))
    o = o * (1.0 / mass)
    lse = top * SCALE + jnp.log(mass)
    return jnp.where(in_circle(lane, turn + HEAD, HEAD), o, lse)


def coarse_blocks(head, recv, back):
    turn = lax.rem(head * HEAD, LANES)
    lane = iota((1, LANES), 1)
    own = jnp.where(in_circle(lane, turn, HEAD), 1.0, 0.0).astype(BF16)
    x = recv[...].reshape(COARSE_ROWS, 2 * LANES)
    step = 256
    below = iota((step, step), 1) <= iota((step, step), 0)
    for b in range(COARSE_ROWS // step):
        def allowed(s):
            last = jnp.where(below, s[:, step * b :], LOWEST)
            return last if b == 0 else jnp.concatenate([s[:, : step * b], last], axis=1)

        q = x[step * b : step * (b + 1), LANES:] * own
        back[step * b : step * (b + 1), :] = attend(q, x[: step * (b + 1)], allowed, iota((step, LANES), 1), turn)


def far_rows(head, grp, recv, far):
    block = 256
    per = block // 8
    chosen = iota((per, block), 1) == iota((per, block), 0) * 8 + head // COARSE
    chosen = jnp.where(chosen, 1.0, 0.0).astype(BF16)
    for b in range(COARSE_ROWS // block):
        x = recv[block // PICKS * b : block // PICKS * (b + 1)].reshape(block, 2 * LANES)
        far[grp, per * b : per * (b + 1), :] = dot(chosen, x).astype(BF16)


def whole_level(head, grp, far, back):
    turn = lax.rem(head * HEAD, LANES)
    lane = iota((1, LANES), 1)
    own = jnp.where(in_circle(lane, turn, HEAD), 1.0, 0.0).astype(BF16)
    keys = far[...].reshape(GRP * FAR, 2 * LANES)
    q = far[grp, :, LANES:] * own

    def allowed(s):
        return jnp.where(iota(s.shape, 1) <= iota(s.shape, 0) + grp * FAR, s, LOWEST)

    lane = iota((FAR, LANES), 1)
    mine = attend(q, keys, allowed, lane, turn)
    rows = pl.ds(head // COARSE, FAR, stride=8)
    other = back[rows, :]
    result = in_circle(lane, turn + HEAD, HEAD)
    l2 = jnp.max(jnp.where(result, LOWEST * 2, other), axis=1, keepdims=True)
    l3 = jnp.max(jnp.where(result, LOWEST * 2, mine), axis=1, keepdims=True)
    best = jnp.maximum(l2, l3)
    e2, e3 = jnp.exp(l2 - best), jnp.exp(l3 - best)
    total = e2 + e3
    back[rows, :] = jnp.where(result, (e2 * other + e3 * mine) / total, best + jnp.log(total))


def merge_group(group, home, o_pick, lse_pick, merged):
    lane = iota((PICKS, LANES), 1)
    tiles_o = [jnp.zeros((PICKS, LANES), F32)] * (SPAN // LANES)
    tiles_l = list(tiles_o)
    for hh in range(GROUP):
        tile, shift, tiles = window(hh)
        m = home[group * GROUP + hh]
        o = pltpu.roll(m, 48, 1)
        at = (shift + 40) % LANES
        lse = jnp.broadcast_to(m[:, at : at + 1], (PICKS, LANES))
        for n in range(tiles):
            here = lane >= shift if n == 0 else lane < shift + HEAD - LANES
            tiles_o[tile + n] = jnp.where(here, o, tiles_o[tile + n])
            tiles_l[tile + n] = jnp.where(here, lse, tiles_l[tile + n])
    for n in range(SPAN // LANES):
        cols = pl.ds(pl.multiple_of(group * SPAN + n * LANES, LANES), LANES)
        l1, l2 = lse_pick[:, cols], tiles_l[n]
        best = jnp.maximum(l1, l2)
        e1, e2 = jnp.exp(l1 - best), jnp.exp(l2 - best)
        merged[:, cols] = ((e1 * o_pick[:, cols] + e2 * tiles_o[n]) / (e1 + e2)).astype(BF16)


def kernel(
    q_hbm, k_hbm, v_hbm, out_t, merged,
    q, k, v, q_pick, o_pick, lse_pick, send, recv, far, back, home,
    in_sem, send_sem, recv_sem, far_send, far_recv, back_send, home_recv,
):
    grp, seq = lax.axis_index("grp"), lax.axis_index("seq")
    head = seq // 2
    owner = lax.rem(seq, 2) == 0

    def loads(group):
        cols = pl.ds(pl.multiple_of(group * SPAN, LANES), SPAN)
        return [
            pltpu.make_async_copy(x.at[:, cols], y.at[:, cols], in_sem.at[group, n])
            for n, (x, y) in enumerate(((q_hbm, q), (k_hbm, k), (v_hbm, v)))
        ]

    for group in range(GROUPS):
        for copy in loads(group):
            copy.start()

    barrier = pltpu.get_barrier_semaphore()

    def greet(s, _):
        @pl.when((s != seq) & (owner | (lax.rem(s, 2) == 0)))
        def _():
            pl.semaphore_signal(barrier, inc=1, device_id=(grp, s), device_id_type=MESH)
        return 0

    lax.fori_loop(0, SEQ, greet, 0)

    @pl.when(owner)
    def _():
        for d in range(1, GRP):
            pl.semaphore_signal(barrier, inc=1, device_id=(lax.rem(grp + d, GRP), seq), device_id_type=MESH)

    gather = jnp.where((iota((PICKS, ROWS), 1) >> 4) == iota((PICKS, ROWS), 0), 1.0, 0.0).astype(BF16)

    def pack(group, _):
        for copy in loads(group):
            copy.wait()
        cols = pl.ds(pl.multiple_of(group * SPAN, LANES), SPAN)
        pack_group(group, q[:, cols], k[:, cols], v[:, cols], group_mask(group), gather, send, q_pick)
        return 0

    lax.fori_loop(0, GROUPS, pack, 0)

    @pl.when(owner)
    def _():
        pl.semaphore_wait(barrier, SEQ - 1 + GRP - 1)

    @pl.when(jnp.logical_not(owner))
    def _():
        pl.semaphore_wait(barrier, HEADS)

    def out(j, _):
        h = lax.rem(head + 1 + j, HEADS)

        @pl.when(2 * h != seq)
        def _():
            pltpu.make_async_remote_copy(
                src_ref=send.at[h], dst_ref=recv.at[seq], send_sem=send_sem, recv_sem=recv_sem,
                device_id=(grp, 2 * h), device_id_type=MESH,
            ).start()

        @pl.when(2 * h == seq)
        def _():
            pltpu.make_async_copy(send.at[h], recv.at[seq], recv_sem).start()
        return 0

    lax.fori_loop(0, HEADS, out, 0)

    def local(group, _):
        cols = pl.ds(pl.multiple_of(group * SPAN, LANES), SPAN)
        local_picks(group, q_pick[group], k[:, cols], v[:, cols], o_pick, lse_pick)
        local_group(group, q[:, cols], k[:, cols], v[:, cols], out_t)
        return 0

    lax.fori_loop(0, GROUPS, local, 0)

    @pl.when(owner)
    def _():
        pltpu.make_async_copy(recv, recv, recv_sem).wait()
        far_rows(head, grp, recv, far)
        for g in range(1, GRP):
            @pl.when(grp < g)
            def _():
                far[g] = jnp.zeros((FAR, 2 * LANES), BF16)

        def far_copy(to):
            return pltpu.make_async_remote_copy(
                src_ref=far.at[grp], dst_ref=far.at[grp], send_sem=far_send.at[to], recv_sem=far_recv.at[grp],
                device_id=(to, seq), device_id_type=MESH,
            )

        for to in range(1, GRP):
            @pl.when(to > grp)
            def _():
                far_copy(to).start()

        coarse_blocks(head, recv, back)
        for g in range(GRP - 1):
            @pl.when(grp > g)
            def _():
                pltpu.make_async_copy(far.at[g], far.at[g], far_recv.at[g]).wait()
        whole_level(head, grp, far, back)

        def home_copy(j, _):
            s = lax.rem(seq + 1 + j, SEQ)
            rows = pl.ds(pl.multiple_of(s * PICKS, PICKS), PICKS)
            pltpu.make_async_remote_copy(
                src_ref=back.at[rows], dst_ref=home.at[head], send_sem=back_send, recv_sem=home_recv,
                device_id=(grp, s), device_id_type=MESH,
            ).start()
            return 0

        lax.fori_loop(0, SEQ - 1, home_copy, 0)
        rows = pl.ds(pl.multiple_of(seq * PICKS, PICKS), PICKS)
        pltpu.make_async_copy(back.at[rows], home.at[head], home_recv).start()

    pltpu.make_async_copy(home, home, home_recv).wait()

    def merge(group, _):
        merge_group(group, home, o_pick, lse_pick, merged)
        return 0

    lax.fori_loop(0, GROUPS, merge, 0)

    @pl.when(owner)
    def _():
        most = send.at[pl.ds(0, HEADS - 1)]
        pltpu.make_async_copy(most, most, send_sem).wait()
        for to in range(1, GRP):
            @pl.when(to > grp)
            def _():
                pltpu.make_async_copy(far.at[0], far.at[0], far_send.at[to]).wait()
        most = back.at[pl.ds(0, (SEQ - 1) * PICKS)]
        pltpu.make_async_copy(most, most, back_send).wait()

    @pl.when(jnp.logical_not(owner))
    def _():
        pltpu.make_async_copy(send, send, send_sem).wait()


def finish_kernel(out_t, merged, out):
    block = out.shape[1]
    shape = (PICKS, COARSE, block)
    o = dot(eye(ROWS), out_t[...], NT).reshape(shape)
    residue = head_of(pl.program_id(0) * block + iota((1, COARSE, block), 2)) & (COARSE - 1)
    chosen = iota((1, COARSE, block), 1) == residue
    rows = merged[...].astype(F32).reshape(PICKS, 1, block)
    out[...] = jnp.where(chosen, rows, o).reshape(ROWS, block).astype(BF16)


def body(queries, key_matrix, value_matrix):
    whole = pl.BlockSpec(memory_space=pltpu.VMEM)
    out_t, merged = pl.pallas_call(
        kernel,
        out_shape=(
            jax.ShapeDtypeStruct((WIDTH, ROWS), BF16),
            jax.ShapeDtypeStruct((PICKS, WIDTH), BF16),
        ),
        in_specs=[pl.BlockSpec(memory_space=pl.ANY)] * 3,
        out_specs=(whole, whole),
        scratch_shapes=[
            pltpu.VMEM((ROWS, WIDTH), BF16),
            pltpu.VMEM((ROWS, WIDTH), BF16),
            pltpu.VMEM((ROWS, WIDTH), BF16),
            pltpu.VMEM((GROUPS, PICKS, SPAN), BF16),
            pltpu.VMEM((PICKS, WIDTH), F32),
            pltpu.VMEM((PICKS, WIDTH), F32),
            pltpu.VMEM((HEADS, PICKS, 2 * LANES), BF16),
            pltpu.VMEM((SEQ, PICKS, 2 * LANES), BF16),
            pltpu.VMEM((GRP, FAR, 2 * LANES), BF16),
            pltpu.VMEM((COARSE_ROWS, LANES), F32),
            pltpu.VMEM((HEADS, PICKS, LANES), F32),
            pltpu.SemaphoreType.DMA((GROUPS, 3)),
            pltpu.SemaphoreType.DMA,
            pltpu.SemaphoreType.DMA,
            pltpu.SemaphoreType.DMA((GRP,)),
            pltpu.SemaphoreType.DMA((GRP,)),
            pltpu.SemaphoreType.DMA,
            pltpu.SemaphoreType.DMA,
        ],
        compiler_params=pltpu.CompilerParams(
            collective_id=0, has_side_effects=True, vmem_limit_bytes=40 * 1024 * 1024
        ),
    )(queries, key_matrix, value_matrix)
    block = 256
    return pl.pallas_call(
        finish_kernel,
        grid=(WIDTH // block,),
        out_shape=jax.ShapeDtypeStruct((ROWS, WIDTH), BF16),
        in_specs=[
            pl.BlockSpec((block, ROWS), lambda j: (j, 0)),
            pl.BlockSpec((PICKS, block), lambda j: (0, j)),
        ],
        out_specs=pl.BlockSpec((ROWS, block), lambda j: (0, j)),
    )(out_t, merged)


def solution(mesh):
    placed = P(("grp", "seq"), None)
    return jax.shard_map(
        body, mesh=mesh, in_specs=(placed,) * 3, out_specs=placed, check_vma=False
    )
```

```python
import functools

import jax
import jax.numpy as jnp
from jax import lax
from jax.experimental import pallas as pl
from jax.experimental.pallas import tpu as pltpu
from jax.sharding import PartitionSpec as P

HEADS = 32
HEAD = 80
WIDTH = HEADS * HEAD
ROWS = 256
COARSE = 16
WHOLE = 128
LANES = 128
GROUP = 8
SPAN = GROUP * HEAD
GROUPS = HEADS // GROUP
SEQ = 64
GRP = 4
PICKS = ROWS // COARSE
COARSE_ROWS = SEQ * PICKS
FAR = ROWS // WHOLE * SEQ
SCALE = HEAD**-0.5
LOG2E = 1.4426950408889634
LOWEST = -1e30
MESH = pl.DeviceIdType.MESH
F32, BF16 = jnp.float32, jnp.bfloat16

NT = (((1,), (1,)), ((), ()))
NN = (((1,), (0,)), ((), ()))


def dot(a, b, dims=NN):
    return lax.dot_general(a, b, dims, preferred_element_type=F32)


def iota(shape, axis):
    return lax.broadcasted_iota(jnp.int32, shape, axis)


def head_of(lane):
    return (lane * 52429) >> 22


def eye(n):
    return jnp.where(iota((n, n), 0) == iota((n, n), 1), 1.0, 0.0).astype(BF16)


def window(hh):
    tile, shift = HEAD * hh // LANES, HEAD * hh % LANES
    return tile, shift, 1 if shift + HEAD <= LANES else 2


def in_circle(lane, start, length):
    return ((lane - start) & (LANES - 1)) < length


def group_mask(group):
    shape = (COARSE, SPAN)
    residue = (head_of(iota(shape, 1)) + group * GROUP) & (COARSE - 1)
    return jnp.where(iota(shape, 0) == residue, 1.0, 0.0).astype(BF16)


def pick(x, mask, gather):
    masked = (x.reshape(PICKS, COARSE, SPAN) * mask[None]).reshape(ROWS, SPAN)
    return dot(gather, masked)


def pack_group(group, q, k, v, mask, gather, send, q_pick):
    lane = iota((PICKS, LANES), 1)
    qp, kp, vp = (pick(x, mask, gather) for x in (q, k, v))
    q_pick[group] = qp.astype(BF16)
    for hh in range(GROUP):
        tile, shift, tiles = window(hh)

        def circle(x):
            first = x[:, LANES * tile : LANES * (tile + 1)]
            if tiles == 1:
                return first
            return jnp.where(lane >= shift, first, x[:, LANES * (tile + 1) : LANES * (tile + 2)])

        own = in_circle(lane, shift, HEAD)
        vc = circle(vp)
        head = group * GROUP + hh
        send[head, :, :LANES] = jnp.where(own, circle(kp), pltpu.roll(vc, HEAD, 1)).astype(BF16)
        send[head, :, LANES:] = jnp.where(own, circle(qp), pltpu.roll(vc, 32, 1)).astype(BF16)


def local_group(group, q, k, v, out):
    unit = eye(LANES)
    half = ROWS // 2
    v_t = jnp.concatenate(
        [dot(unit, v[:, LANES * j : LANES * (j + 1)], NT).astype(BF16) for j in range(SPAN // LANES)], axis=0
    )
    allowed = iota((half, half), 0) <= iota((half, half), 1)
    parts = []
    for hh in range(GROUP):
        tile, shift, tiles = window(hh)
        cols = slice(LANES * tile, LANES * (tile + tiles))
        lane = iota((1, LANES * tiles), 1)
        own = jnp.where((lane >= shift) & (lane < shift + HEAD), 1.0, 0.0).astype(BF16)
        s = dot(k[:, cols], q[:, cols] * own, NT)
        s00 = jnp.where(allowed, s[:half, :half], LOWEST)
        s01 = s[:half, half:]
        s11 = jnp.where(allowed, s[half:, half:], LOWEST)
        top0 = jnp.max(s00, axis=0, keepdims=True)
        top1 = jnp.maximum(jnp.max(s01, axis=0, keepdims=True), jnp.max(s11, axis=0, keepdims=True))
        w00 = jnp.exp2((s00 - top0) * (SCALE * LOG2E))
        w01 = jnp.exp2((s01 - top1) * (SCALE * LOG2E))
        w11 = jnp.exp2((s11 - top1) * (SCALE * LOG2E))
        mass0 = jnp.sum(w00, axis=0, keepdims=True)
        mass1 = jnp.sum(w01, axis=0, keepdims=True) + jnp.sum(w11, axis=0, keepdims=True)
        w = jnp.concatenate(
            [
                jnp.concatenate([w00.astype(BF16), w01.astype(BF16)], axis=1),
                jnp.concatenate([jnp.zeros((half, half), BF16), w11.astype(BF16)], axis=1),
            ],
            axis=0,
        )
        o = dot(v_t[HEAD * hh : HEAD * (hh + 1)], w)
        o = o * (1.0 / jnp.concatenate([mass0, mass1], axis=1))
        parts.append(o.astype(BF16))
    turned = jnp.concatenate(parts, axis=0)
    unit = eye(ROWS)
    for j in range(SPAN // LANES):
        cols = pl.ds(pl.multiple_of(group * SPAN + LANES * j, LANES), LANES)
        out[:, cols] = dot(unit, turned[LANES * j : LANES * (j + 1)], NT).astype(BF16)


def local_picks(group, q_pick, k, v, o_pick, lse_pick):
    shape = (GROUP * PICKS, SPAN)
    own = (iota(shape, 0) >> 4) == head_of(iota(shape, 1))
    q = jnp.concatenate([q_pick] * GROUP, axis=0) * jnp.where(own, 1.0, 0.0).astype(BF16)
    s = dot(q, k, NT)
    row, key = iota(s.shape, 0), iota(s.shape, 1)
    residue = ((row >> 4) + group * GROUP) & (COARSE - 1)
    s = jnp.where(key <= (row & (PICKS - 1)) * COARSE + residue, s, LOWEST)
    top = jnp.max(s, axis=1, keepdims=True)
    w = jnp.exp2((s - top) * (SCALE * LOG2E))
    mass = jnp.sum(w, axis=1, keepdims=True)
    o = dot(w.astype(BF16), v) * (1.0 / mass)
    lse = top * SCALE + jnp.log(mass)
    cols = pl.ds(pl.multiple_of(group * SPAN, LANES), SPAN)
    o_pick[:, cols] = jnp.sum(jnp.where(own, o, 0.0).reshape(GROUP, PICKS, SPAN), axis=0)
    lse_pick[:, cols] = jnp.sum(jnp.where(own, lse, 0.0).reshape(GROUP, PICKS, SPAN), axis=0)


def attend(q, keys, allowed, lane, turn):
    s = dot(q, keys[:, :LANES], NT)
    s = allowed(s)
    top = jnp.max(s, axis=1, keepdims=True)
    w = jnp.exp2((s - top) * (SCALE * LOG2E))
    mass = jnp.sum(w, axis=1, keepdims=True)
    both = dot(w.astype(BF16), keys)
    o = jnp.where(in_circle(lane, turn + HEAD, 48), both[:, :LANES], pltpu.roll(both[:, LANES:], 48, 1))
    o = o * (1.0 / mass)
    lse = top * SCALE + jnp.log(mass)
    return jnp.where(in_circle(lane, turn + HEAD, HEAD), o, lse)


def coarse_blocks(head, recv, back):
    turn = lax.rem(head * HEAD, LANES)
    lane = iota((1, LANES), 1)
    own = jnp.where(in_circle(lane, turn, HEAD), 1.0, 0.0).astype(BF16)
    x = recv[...].reshape(COARSE_ROWS, 2 * LANES)
    step = 256
    below = iota((step, step), 1) <= iota((step, step), 0)
    for b in range(COARSE_ROWS // step):
        def allowed(s):
            last = jnp.where(below, s[:, step * b :], LOWEST)
            return last if b == 0 else jnp.concatenate([s[:, : step * b], last], axis=1)

        q = x[step * b : step * (b + 1), LANES:] * own
        back[step * b : step * (b + 1), :] = attend(q, x[: step * (b + 1)], allowed, iota((step, LANES), 1), turn)


def far_rows(head, grp, recv, far):
    block = 256
    per = block // 8
    chosen = iota((per, block), 1) == iota((per, block), 0) * 8 + head // COARSE
    chosen = jnp.where(chosen, 1.0, 0.0).astype(BF16)
    for b in range(COARSE_ROWS // block):
        x = recv[block // PICKS * b : block // PICKS * (b + 1)].reshape(block, 2 * LANES)
        far[grp, per * b : per * (b + 1), :] = dot(chosen, x).astype(BF16)


def whole_level(head, grp, far, back):
    turn = lax.rem(head * HEAD, LANES)
    lane = iota((1, LANES), 1)
    own = jnp.where(in_circle(lane, turn, HEAD), 1.0, 0.0).astype(BF16)
    keys = far[...].reshape(GRP * FAR, 2 * LANES)
    q = far[grp, :, LANES:] * own

    def allowed(s):
        return jnp.where(iota(s.shape, 1) <= iota(s.shape, 0) + grp * FAR, s, LOWEST)

    lane = iota((FAR, LANES), 1)
    mine = attend(q, keys, allowed, lane, turn)
    rows = pl.ds(head // COARSE, FAR, stride=8)
    other = back[rows, :]
    result = in_circle(lane, turn + HEAD, HEAD)
    l2 = jnp.max(jnp.where(result, LOWEST * 2, other), axis=1, keepdims=True)
    l3 = jnp.max(jnp.where(result, LOWEST * 2, mine), axis=1, keepdims=True)
    best = jnp.maximum(l2, l3)
    e2, e3 = jnp.exp(l2 - best), jnp.exp(l3 - best)
    total = e2 + e3
    back[rows, :] = jnp.where(result, (e2 * other + e3 * mine) / total, best + jnp.log(total))


def merge_group(group, home, o_pick, lse_pick, out):
    lane = iota((PICKS, LANES), 1)
    tiles_o = [jnp.zeros((PICKS, LANES), F32)] * (SPAN // LANES)
    tiles_l = list(tiles_o)
    for hh in range(GROUP):
        tile, shift, tiles = window(hh)
        m = home[group * GROUP + hh]
        o = pltpu.roll(m, 48, 1)
        at = (shift + 40) % LANES
        lse = jnp.broadcast_to(m[:, at : at + 1], (PICKS, LANES))
        for n in range(tiles):
            here = lane >= shift if n == 0 else lane < shift + HEAD - LANES
            tiles_o[tile + n] = jnp.where(here, o, tiles_o[tile + n])
            tiles_l[tile + n] = jnp.where(here, lse, tiles_l[tile + n])
    for n in range(SPAN // LANES):
        cols = pl.ds(pl.multiple_of(group * SPAN + n * LANES, LANES), LANES)
        l1, l2 = lse_pick[:, cols], tiles_l[n]
        best = jnp.maximum(l1, l2)
        e1, e2 = jnp.exp(l1 - best), jnp.exp(l2 - best)
        merged = (e1 * o_pick[:, cols] + e2 * tiles_o[n]) / (e1 + e2)
        shape = (PICKS, COARSE, LANES)
        residue = head_of(iota((1, COARSE, LANES), 2) + (group * SPAN + n * LANES)) & (COARSE - 1)
        chosen = iota((1, COARSE, LANES), 1) == residue
        rows = jnp.where(chosen, merged.reshape(PICKS, 1, LANES), out[:, cols].reshape(shape).astype(F32))
        out[:, cols] = rows.reshape(ROWS, LANES).astype(BF16)


def kernel(
    q_hbm, k_hbm, v_hbm, out,
    q, k, v, q_pick, o_pick, lse_pick, send, recv, far, back, home,
    in_sem, send_sem, recv_sem, far_send, far_recv, back_send, home_recv,
):
    grp, seq = lax.axis_index("grp"), lax.axis_index("seq")
    head = seq // 2
    owner = lax.rem(seq, 2) == 0

    def loads(group):
        cols = pl.ds(pl.multiple_of(group * SPAN, LANES), SPAN)
        return [
            pltpu.make_async_copy(x.at[:, cols], y.at[:, cols], in_sem.at[group, n])
            for n, (x, y) in enumerate(((q_hbm, q), (k_hbm, k), (v_hbm, v)))
        ]

    for group in range(GROUPS):
        for copy in loads(group):
            copy.start()

    barrier = pltpu.get_barrier_semaphore()

    def greet(s, _):
        @pl.when((s != seq) & (owner | (lax.rem(s, 2) == 0)))
        def _():
            pl.semaphore_signal(barrier, inc=1, device_id=(grp, s), device_id_type=MESH)
        return 0

    lax.fori_loop(0, SEQ, greet, 0)

    @pl.when(owner)
    def _():
        for d in range(1, GRP):
            pl.semaphore_signal(barrier, inc=1, device_id=(lax.rem(grp + d, GRP), seq), device_id_type=MESH)

    gather = jnp.where((iota((PICKS, ROWS), 1) >> 4) == iota((PICKS, ROWS), 0), 1.0, 0.0).astype(BF16)

    def pack(group, _):
        for copy in loads(group):
            copy.wait()
        cols = pl.ds(pl.multiple_of(group * SPAN, LANES), SPAN)
        pack_group(group, q[:, cols], k[:, cols], v[:, cols], group_mask(group), gather, send, q_pick)
        return 0

    lax.fori_loop(0, GROUPS, pack, 0)

    @pl.when(owner)
    def _():
        pl.semaphore_wait(barrier, SEQ - 1 + GRP - 1)

    @pl.when(jnp.logical_not(owner))
    def _():
        pl.semaphore_wait(barrier, HEADS)

    def share(j, _):
        h = lax.rem(head + 1 + j, HEADS)

        @pl.when(2 * h != seq)
        def _():
            pltpu.make_async_remote_copy(
                src_ref=send.at[h], dst_ref=recv.at[seq], send_sem=send_sem, recv_sem=recv_sem,
                device_id=(grp, 2 * h), device_id_type=MESH,
            ).start()

        @pl.when(2 * h == seq)
        def _():
            pltpu.make_async_copy(send.at[h], recv.at[seq], recv_sem).start()
        return 0

    lax.fori_loop(0, HEADS, share, 0)

    def local(group, _):
        cols = pl.ds(pl.multiple_of(group * SPAN, LANES), SPAN)
        local_picks(group, q_pick[group], k[:, cols], v[:, cols], o_pick, lse_pick)
        local_group(group, q[:, cols], k[:, cols], v[:, cols], out)
        return 0

    lax.fori_loop(0, GROUPS, local, 0)

    @pl.when(owner)
    def _():
        pltpu.make_async_copy(recv, recv, recv_sem).wait()
        far_rows(head, grp, recv, far)
        for g in range(1, GRP):
            @pl.when(grp < g)
            def _():
                far[g] = jnp.zeros((FAR, 2 * LANES), BF16)

        def far_copy(to):
            return pltpu.make_async_remote_copy(
                src_ref=far.at[grp], dst_ref=far.at[grp], send_sem=far_send.at[to], recv_sem=far_recv.at[grp],
                device_id=(to, seq), device_id_type=MESH,
            )

        for to in range(1, GRP):
            @pl.when(to > grp)
            def _():
                far_copy(to).start()

        coarse_blocks(head, recv, back)
        for g in range(GRP - 1):
            @pl.when(grp > g)
            def _():
                pltpu.make_async_copy(far.at[g], far.at[g], far_recv.at[g]).wait()
        whole_level(head, grp, far, back)

        def home_copy(j, _):
            s = lax.rem(seq + 1 + j, SEQ)
            rows = pl.ds(pl.multiple_of(s * PICKS, PICKS), PICKS)
            pltpu.make_async_remote_copy(
                src_ref=back.at[rows], dst_ref=home.at[head], send_sem=back_send, recv_sem=home_recv,
                device_id=(grp, s), device_id_type=MESH,
            ).start()
            return 0

        lax.fori_loop(0, SEQ - 1, home_copy, 0)
        rows = pl.ds(pl.multiple_of(seq * PICKS, PICKS), PICKS)
        pltpu.make_async_copy(back.at[rows], home.at[head], home_recv).start()

    pltpu.make_async_copy(home, home, home_recv).wait()

    def merge(group, _):
        merge_group(group, home, o_pick, lse_pick, out)
        return 0

    lax.fori_loop(0, GROUPS, merge, 0)

    @pl.when(owner)
    def _():
        most = send.at[pl.ds(0, HEADS - 1)]
        pltpu.make_async_copy(most, most, send_sem).wait()
        for to in range(1, GRP):
            @pl.when(to > grp)
            def _():
                pltpu.make_async_copy(far.at[0], far.at[0], far_send.at[to]).wait()
        most = back.at[pl.ds(0, (SEQ - 1) * PICKS)]
        pltpu.make_async_copy(most, most, back_send).wait()

    @pl.when(jnp.logical_not(owner))
    def _():
        pltpu.make_async_copy(send, send, send_sem).wait()


def body(queries, key_matrix, value_matrix):
    return pl.pallas_call(
        kernel,
        out_shape=jax.ShapeDtypeStruct((ROWS, WIDTH), BF16),
        in_specs=[pl.BlockSpec(memory_space=pltpu.HBM)] * 3,
        out_specs=pl.BlockSpec(memory_space=pltpu.VMEM),
        scratch_shapes=[
            pltpu.VMEM((ROWS, WIDTH), BF16),
            pltpu.VMEM((ROWS, WIDTH), BF16),
            pltpu.VMEM((ROWS, WIDTH), BF16),
            pltpu.VMEM((GROUPS, PICKS, SPAN), BF16),
            pltpu.VMEM((PICKS, WIDTH), F32),
            pltpu.VMEM((PICKS, WIDTH), F32),
            pltpu.VMEM((HEADS, PICKS, 2 * LANES), BF16),
            pltpu.VMEM((SEQ, PICKS, 2 * LANES), BF16),
            pltpu.VMEM((GRP, FAR, 2 * LANES), BF16),
            pltpu.VMEM((COARSE_ROWS, LANES), F32),
            pltpu.VMEM((HEADS, PICKS, LANES), F32),
            pltpu.SemaphoreType.DMA((GROUPS, 3)),
            pltpu.SemaphoreType.DMA,
            pltpu.SemaphoreType.DMA,
            pltpu.SemaphoreType.DMA((GRP,)),
            pltpu.SemaphoreType.DMA((GRP,)),
            pltpu.SemaphoreType.DMA,
            pltpu.SemaphoreType.DMA,
        ],
        compiler_params=pltpu.CompilerParams(
            collective_id=0, has_side_effects=True, vmem_limit_bytes=48 * 1024 * 1024
        ),
    )(*(pltpu.with_memory_space_constraint(x, pltpu.HBM) for x in (queries, key_matrix, value_matrix)))


def solution(mesh):
    placed = P(("grp", "seq"), None)
    return jax.shard_map(
        body, mesh=mesh, in_specs=(placed,) * 3, out_specs=placed, check_vma=False
    )
```

```python
import functools

import jax
import jax.numpy as jnp
from jax import lax
from jax.experimental import pallas as pl
from jax.experimental.pallas import tpu as pltpu
from jax.sharding import PartitionSpec as P

HEADS = 32
HEAD = 80
WIDTH = HEADS * HEAD
ROWS = 256
COARSE = 16
WHOLE = 128
LANES = 128
GROUP = 8
SPAN = GROUP * HEAD
GROUPS = HEADS // GROUP
SEQ = 64
GRP = 4
PICKS = ROWS // COARSE
COARSE_ROWS = SEQ * PICKS
HALF_ROWS = COARSE_ROWS // 2
FAR = ROWS // WHOLE * SEQ // 2
SCALE = HEAD**-0.5
LOG2E = 1.4426950408889634
LOWEST = -1e30
MESH = pl.DeviceIdType.MESH
F32, BF16 = jnp.float32, jnp.bfloat16

NT = (((1,), (1,)), ((), ()))
NN = (((1,), (0,)), ((), ()))


def dot(a, b, dims=NN):
    return lax.dot_general(a, b, dims, preferred_element_type=F32)


def iota(shape, axis):
    return lax.broadcasted_iota(jnp.int32, shape, axis)


def head_of(lane):
    return (lane * 52429) >> 22


def eye(n):
    return jnp.where(iota((n, n), 0) == iota((n, n), 1), 1.0, 0.0).astype(BF16)


def window(hh):
    tile, shift = HEAD * hh // LANES, HEAD * hh % LANES
    return tile, shift, 1 if shift + HEAD <= LANES else 2


def in_circle(lane, start, length):
    return ((lane - start) & (LANES - 1)) < length


def group_mask(group):
    shape = (COARSE, SPAN)
    residue = (head_of(iota(shape, 1)) + group * GROUP) & (COARSE - 1)
    return jnp.where(iota(shape, 0) == residue, 1.0, 0.0).astype(BF16)


def pick(x, mask, gather):
    masked = (x.reshape(PICKS, COARSE, SPAN) * mask[None]).reshape(ROWS, SPAN)
    return dot(gather, masked)


def pack_group(group, q, k, v, mask, gather, send, q_pick):
    lane = iota((PICKS, LANES), 1)
    qp, kp, vp = (pick(x, mask, gather) for x in (q, k, v))
    q_pick[group] = qp.astype(BF16)
    for hh in range(GROUP):
        tile, shift, tiles = window(hh)

        def circle(x):
            first = x[:, LANES * tile : LANES * (tile + 1)]
            if tiles == 1:
                return first
            return jnp.where(lane >= shift, first, x[:, LANES * (tile + 1) : LANES * (tile + 2)])

        own = in_circle(lane, shift, HEAD)
        vc = circle(vp)
        head = group * GROUP + hh
        send[head, :, :LANES] = jnp.where(own, circle(kp), pltpu.roll(vc, HEAD, 1)).astype(BF16)
        send[head, :, LANES:] = jnp.where(own, circle(qp), pltpu.roll(vc, 32, 1)).astype(BF16)


def local_group(group, q, k, v, out):
    unit = eye(LANES)
    half = ROWS // 2
    v_t = jnp.concatenate(
        [dot(unit, v[:, LANES * j : LANES * (j + 1)], NT).astype(BF16) for j in range(SPAN // LANES)], axis=0
    )
    allowed = iota((half, half), 0) <= iota((half, half), 1)
    parts = []
    for hh in range(GROUP):
        tile, shift, tiles = window(hh)
        cols = slice(LANES * tile, LANES * (tile + tiles))
        lane = iota((1, LANES * tiles), 1)
        own = jnp.where((lane >= shift) & (lane < shift + HEAD), 1.0, 0.0).astype(BF16)
        s = dot(k[:, cols], q[:, cols] * own, NT)
        s00 = jnp.where(allowed, s[:half, :half], LOWEST)
        s01 = s[:half, half:]
        s11 = jnp.where(allowed, s[half:, half:], LOWEST)
        top0 = jnp.max(s00, axis=0, keepdims=True)
        top1 = jnp.maximum(jnp.max(s01, axis=0, keepdims=True), jnp.max(s11, axis=0, keepdims=True))
        w00 = jnp.exp2((s00 - top0) * (SCALE * LOG2E))
        w01 = jnp.exp2((s01 - top1) * (SCALE * LOG2E))
        w11 = jnp.exp2((s11 - top1) * (SCALE * LOG2E))
        mass0 = jnp.sum(w00, axis=0, keepdims=True)
        mass1 = jnp.sum(w01, axis=0, keepdims=True) + jnp.sum(w11, axis=0, keepdims=True)
        w = jnp.concatenate(
            [
                jnp.concatenate([w00.astype(BF16), w01.astype(BF16)], axis=1),
                jnp.concatenate([jnp.zeros((half, half), BF16), w11.astype(BF16)], axis=1),
            ],
            axis=0,
        )
        o = dot(v_t[HEAD * hh : HEAD * (hh + 1)], w)
        o = o * (1.0 / jnp.concatenate([mass0, mass1], axis=1))
        parts.append(o.astype(BF16))
    turned = jnp.concatenate(parts, axis=0)
    unit = eye(ROWS)
    for j in range(SPAN // LANES):
        cols = pl.ds(pl.multiple_of(group * SPAN + LANES * j, LANES), LANES)
        out[:, cols] = dot(unit, turned[LANES * j : LANES * (j + 1)], NT).astype(BF16)


def local_picks(group, q_pick, k, v, o_pick, lse_pick):
    shape = (GROUP * PICKS, SPAN)
    own = (iota(shape, 0) >> 4) == head_of(iota(shape, 1))
    q = jnp.concatenate([q_pick] * GROUP, axis=0) * jnp.where(own, 1.0, 0.0).astype(BF16)
    s = dot(q, k, NT)
    row, key = iota(s.shape, 0), iota(s.shape, 1)
    residue = ((row >> 4) + group * GROUP) & (COARSE - 1)
    s = jnp.where(key <= (row & (PICKS - 1)) * COARSE + residue, s, LOWEST)
    top = jnp.max(s, axis=1, keepdims=True)
    w = jnp.exp2((s - top) * (SCALE * LOG2E))
    mass = jnp.sum(w, axis=1, keepdims=True)
    o = dot(w.astype(BF16), v) * (1.0 / mass)
    lse = top * SCALE + jnp.log(mass)
    cols = pl.ds(pl.multiple_of(group * SPAN, LANES), SPAN)
    o_pick[:, cols] = jnp.sum(jnp.where(own, o, 0.0).reshape(GROUP, PICKS, SPAN), axis=0)
    lse_pick[:, cols] = jnp.sum(jnp.where(own, lse, 0.0).reshape(GROUP, PICKS, SPAN), axis=0)


def attend(q, parts, lane, turn):
    scores = [hide(dot(q, keys[:, :LANES], NT)) for keys, hide in parts]
    top = functools.reduce(jnp.maximum, [jnp.max(s, axis=1, keepdims=True) for s in scores])
    weights = [jnp.exp2((s - top) * (SCALE * LOG2E)) for s in scores]
    mass = sum(jnp.sum(w, axis=1, keepdims=True) for w in weights)
    both = sum(dot(w.astype(BF16), keys) for w, (keys, _) in zip(weights, parts))
    o = jnp.where(in_circle(lane, turn + HEAD, 48), both[:, :LANES], pltpu.roll(both[:, LANES:], 48, 1))
    o = o * (1.0 / mass)
    lse = top * SCALE + jnp.log(mass)
    return jnp.where(in_circle(lane, turn + HEAD, HEAD), o, lse)


def place(p, half):
    return (p >> 3) * 16 + half * 8 + (p & 7)


def coarse_blocks(head, half, near, other, back):
    turn = lax.rem(head * HEAD, LANES)
    own = jnp.where(in_circle(iota((1, LANES), 1), turn, HEAD), 1.0, 0.0).astype(BF16)
    step = 128
    below = iota((step, step), 1) <= iota((step, step), 0)
    x = near[...].reshape(HALF_ROWS, 2 * LANES)
    y = other[...].reshape(HALF_ROWS, 2 * LANES)
    for b in range(HALF_ROWS // step):
        start = b * step

        def last_hidden(s):
            last = jnp.where(below, s[:, start:], LOWEST)
            return last if b == 0 else jnp.concatenate([s[:, :start], last], axis=1)

        parts = [(x[: start + step], last_hidden)]
        if b + half > 0:
            parts.append((y[: start + half * step], lambda s: s))
        q = x[start : start + step, LANES:] * own
        back[start : start + step, :] = attend(q, parts, iota((step, LANES), 1), turn)


def far_rows(head, half, grp, recv, far):
    block = 256
    per = block // 8
    chosen = iota((per, block), 1) == iota((per, block), 0) * 8 + head // COARSE
    chosen = jnp.where(chosen, 1.0, 0.0).astype(BF16)
    for b in range(HALF_ROWS // block):
        x = recv[block // PICKS * b : block // PICKS * (b + 1)].reshape(block, 2 * LANES)
        far[grp, half, per * b : per * (b + 1), :] = dot(chosen, x).astype(BF16)


def far_place(r):
    return (r >> 4) * 32 + (r & 15)


def whole_level(head, half, grp, far, back):
    turn = lax.rem(head * HEAD, LANES)
    own = jnp.where(in_circle(iota((1, LANES), 1), turn, HEAD), 1.0, 0.0).astype(BF16)
    keys = far[...].reshape(GRP * 2 * FAR, 2 * LANES)
    q = far[grp, half, :, LANES:] * own

    def hide(s):
        row, col = iota(s.shape, 0), iota(s.shape, 1)
        row = grp * (2 * FAR) + half * 16 + far_place(row)
        col = (col >> 7) * (2 * FAR) + ((col >> 6) & 1) * 16 + far_place(col & (FAR - 1))
        return jnp.where(col <= row, s, LOWEST)

    lane = iota((FAR, LANES), 1)
    mine = attend(q, [(keys, hide)], lane, turn)
    rows = pl.ds(head // COARSE, FAR, stride=8)
    other = back[rows, :]
    result = in_circle(lane, turn + HEAD, HEAD)
    l2 = jnp.max(jnp.where(result, LOWEST * 2, other), axis=1, keepdims=True)
    l3 = jnp.max(jnp.where(result, LOWEST * 2, mine), axis=1, keepdims=True)
    best = jnp.maximum(l2, l3)
    e2, e3 = jnp.exp(l2 - best), jnp.exp(l3 - best)
    total = e2 + e3
    back[rows, :] = jnp.where(result, (e2 * other + e3 * mine) / total, best + jnp.log(total))


def merge_group(group, home, o_pick, lse_pick, out):
    lane = iota((PICKS, LANES), 1)
    tiles_o = [jnp.zeros((PICKS, LANES), F32)] * (SPAN // LANES)
    tiles_l = list(tiles_o)
    for hh in range(GROUP):
        tile, shift, tiles = window(hh)
        m = home[group * GROUP + hh]
        o = pltpu.roll(m, 48, 1)
        at = (shift + 40) % LANES
        lse = jnp.broadcast_to(m[:, at : at + 1], (PICKS, LANES))
        for n in range(tiles):
            here = lane >= shift if n == 0 else lane < shift + HEAD - LANES
            tiles_o[tile + n] = jnp.where(here, o, tiles_o[tile + n])
            tiles_l[tile + n] = jnp.where(here, lse, tiles_l[tile + n])
    for n in range(SPAN // LANES):
        cols = pl.ds(pl.multiple_of(group * SPAN + n * LANES, LANES), LANES)
        l1, l2 = lse_pick[:, cols], tiles_l[n]
        best = jnp.maximum(l1, l2)
        e1, e2 = jnp.exp(l1 - best), jnp.exp(l2 - best)
        merged = (e1 * o_pick[:, cols] + e2 * tiles_o[n]) / (e1 + e2)
        shape = (PICKS, COARSE, LANES)
        residue = head_of(iota((1, COARSE, LANES), 2) + (group * SPAN + n * LANES)) & (COARSE - 1)
        chosen = iota((1, COARSE, LANES), 1) == residue
        rows = jnp.where(chosen, merged.reshape(PICKS, 1, LANES), out[:, cols].reshape(shape).astype(F32))
        out[:, cols] = rows.reshape(ROWS, LANES).astype(BF16)


def kernel(
    q_hbm, k_hbm, v_hbm, out,
    q, k, v, q_pick, o_pick, lse_pick, send, near, other, far, back, home,
    in_sem, send_sem, recv_sem, far_send, far_recv, back_send, home_recv,
):
    grp, seq = lax.axis_index("grp"), lax.axis_index("seq")
    half = (seq >> 3) & 1
    head = (seq >> 4) * 8 + (seq & 7)
    late = (half == 1) & (head >= HEADS - 8)

    barrier = pltpu.get_barrier_semaphore()

    def greet(j, _):
        p = (head + j) & (HEADS - 1)
        pl.semaphore_signal(barrier, inc=1, device_id=(grp, place(p, 1 - half)), device_id_type=MESH)
        return 0

    def greet_near(j, _):
        p = (head + j) & (HEADS - 1)
        pl.semaphore_signal(barrier, inc=1, device_id=(grp, place(p, half)), device_id_type=MESH)
        return 0

    lax.fori_loop(0, HEADS, greet, 0)
    for d in range(1, GRP):
        for h in (1 - half, half):
            pl.semaphore_signal(
                barrier, inc=1, device_id=(lax.rem(grp + d, GRP), place(head, h)), device_id_type=MESH
            )
    lax.fori_loop(1, HEADS, greet_near, 0)

    def loads(group):
        cols = pl.ds(pl.multiple_of(group * SPAN, LANES), SPAN)
        return [
            pltpu.make_async_copy(x.at[:, cols], y.at[:, cols], in_sem.at[group, n])
            for n, (x, y) in enumerate(((q_hbm, q), (k_hbm, k), (v_hbm, v)))
        ]

    for group in range(GROUPS):
        for copy in loads(group):
            copy.start()

    gather = jnp.where((iota((PICKS, ROWS), 1) >> 4) == iota((PICKS, ROWS), 0), 1.0, 0.0).astype(BF16)

    def pack(group, _):
        for copy in loads(group):
            copy.wait()
        cols = pl.ds(pl.multiple_of(group * SPAN, LANES), SPAN)
        pack_group(group, q[:, cols], k[:, cols], v[:, cols], group_mask(group), gather, send, q_pick)
        return 0

    lax.fori_loop(0, GROUPS, pack, 0)

    pl.semaphore_wait(barrier, SEQ - 1 + 2 * (GRP - 1))

    def across(j, _):
        h = (head + j) & (HEADS - 1)
        pltpu.make_async_remote_copy(
            src_ref=send.at[h], dst_ref=other.at[head], send_sem=send_sem, recv_sem=recv_sem.at[1],
            device_id=(grp, place(h, 1 - half)), device_id_type=MESH,
        ).start()
        return 0

    def beside(j, _):
        h = (head + j) & (HEADS - 1)
        pltpu.make_async_remote_copy(
            src_ref=send.at[h], dst_ref=near.at[head], send_sem=send_sem, recv_sem=recv_sem.at[0],
            device_id=(grp, place(h, half)), device_id_type=MESH,
        ).start()
        return 0

    @pl.when(jnp.logical_not(late))
    def _():
        lax.fori_loop(0, HEADS, across, 0)

    lax.fori_loop(1, HEADS, beside, 0)
    pltpu.make_async_copy(send.at[head], near.at[head], recv_sem.at[0]).start()

    def local(group, _):
        cols = pl.ds(pl.multiple_of(group * SPAN, LANES), SPAN)
        local_picks(group, q_pick[group], k[:, cols], v[:, cols], o_pick, lse_pick)
        local_group(group, q[:, cols], k[:, cols], v[:, cols], out)
        return 0

    lax.fori_loop(0, GROUPS // 2, local, 0)

    for g in range(1, GRP):
        @pl.when(grp < g)
        def _():
            far[g] = jnp.zeros((2, FAR, 2 * LANES), BF16)

    @pl.when(half == 0)
    def _():
        other[HEADS - 8 :] = jnp.zeros((8, PICKS, 2 * LANES), BF16)

    pltpu.make_async_copy(near, near, recv_sem.at[0]).wait()
    far_rows(head, half, grp, near, far)

    def far_copy(to, h):
        return pltpu.make_async_remote_copy(
            src_ref=far.at[grp, half], dst_ref=far.at[grp, half],
            send_sem=far_send.at[to, h], recv_sem=far_recv.at[grp, half],
            device_id=(to, place(head, h)), device_id_type=MESH,
        )

    for to in range(1, GRP):
        @pl.when(to > grp)
        def _():
            far_copy(to, 1 - half).start()
            far_copy(to, half).start()

    lax.fori_loop(GROUPS // 2, GROUPS, local, 0)

    @pl.when(half == 0)
    def _():
        part = other.at[pl.ds(0, HEADS - 8)]
        pltpu.make_async_copy(part, part, recv_sem.at[1]).wait()
        far_rows(head, 1, grp, other, far)
        coarse_blocks(head, 0, near, other, back)

    @pl.when(half == 1)
    def _():
        pltpu.make_async_copy(other, other, recv_sem.at[1]).wait()
        far_rows(head, 0, grp, other, far)
        coarse_blocks(head, 1, near, other, back)

    for g in range(GRP - 1):
        @pl.when(grp > g)
        def _():
            for h in range(2):
                pltpu.make_async_copy(far.at[g, h], far.at[g, h], far_recv.at[g, h]).wait()

    whole_level(head, half, grp, far, back)

    def home_copy(j, _):
        p = (head + j) & (HEADS - 1)
        rows = pl.ds(pl.multiple_of(p * PICKS, PICKS), PICKS)
        pltpu.make_async_remote_copy(
            src_ref=back.at[rows], dst_ref=home.at[head], send_sem=back_send, recv_sem=home_recv.at[head // GROUP],
            device_id=(grp, place(p, half)), device_id_type=MESH,
        ).start()
        return 0

    lax.fori_loop(1, HEADS, home_copy, 0)
    rows = pl.ds(pl.multiple_of(head * PICKS, PICKS), PICKS)
    pltpu.make_async_copy(back.at[rows], home.at[head], home_recv.at[head // GROUP]).start()

    def merge(group, _):
        part = home.at[pl.ds(group * GROUP, GROUP)]
        pltpu.make_async_copy(part, part, home_recv.at[group]).wait()
        merge_group(group, home, o_pick, lse_pick, out)
        return 0

    lax.fori_loop(0, GROUPS, merge, 0)

    most = send.at[pl.ds(0, HEADS - 1)]
    pltpu.make_async_copy(most, most, send_sem).wait()

    @pl.when(jnp.logical_not(late))
    def _():
        pltpu.make_async_copy(send, send, send_sem).wait()

    for to in range(1, GRP):
        @pl.when(to > grp)
        def _():
            for h in range(2):
                pltpu.make_async_copy(far.at[0, 0], far.at[0, 0], far_send.at[to, h]).wait()
    most = back.at[pl.ds(0, (HEADS - 1) * PICKS)]
    pltpu.make_async_copy(most, most, back_send).wait()


def body(queries, key_matrix, value_matrix):
    return pl.pallas_call(
        kernel,
        out_shape=jax.ShapeDtypeStruct((ROWS, WIDTH), BF16),
        in_specs=[pl.BlockSpec(memory_space=pltpu.HBM)] * 3,
        out_specs=pl.BlockSpec(memory_space=pltpu.VMEM),
        scratch_shapes=[
            pltpu.VMEM((ROWS, WIDTH), BF16),
            pltpu.VMEM((ROWS, WIDTH), BF16),
            pltpu.VMEM((ROWS, WIDTH), BF16),
            pltpu.VMEM((GROUPS, PICKS, SPAN), BF16),
            pltpu.VMEM((PICKS, WIDTH), F32),
            pltpu.VMEM((PICKS, WIDTH), F32),
            pltpu.VMEM((HEADS, PICKS, 2 * LANES), BF16),
            pltpu.VMEM((HEADS, PICKS, 2 * LANES), BF16),
            pltpu.VMEM((HEADS, PICKS, 2 * LANES), BF16),
            pltpu.VMEM((GRP, 2, FAR, 2 * LANES), BF16),
            pltpu.VMEM((HALF_ROWS, LANES), F32),
            pltpu.VMEM((HEADS, PICKS, LANES), F32),
            pltpu.SemaphoreType.DMA((GROUPS, 3)),
            pltpu.SemaphoreType.DMA,
            pltpu.SemaphoreType.DMA((2,)),
            pltpu.SemaphoreType.DMA((GRP, 2)),
            pltpu.SemaphoreType.DMA((GRP, 2)),
            pltpu.SemaphoreType.DMA,
            pltpu.SemaphoreType.DMA((GROUPS,)),
        ],
        compiler_params=pltpu.CompilerParams(
            collective_id=0, has_side_effects=True, vmem_limit_bytes=48 * 1024 * 1024
        ),
    )(*(pltpu.with_memory_space_constraint(x, pltpu.HBM) for x in (queries, key_matrix, value_matrix)))


def solution(mesh):
    placed = P(("grp", "seq"), None)
    return jax.shard_map(
        body, mesh=mesh, in_specs=(placed,) * 3, out_specs=placed, check_vma=False
    )
```

```python
import functools

import jax
import jax.numpy as jnp
from jax import lax
from jax.experimental import pallas as pl
from jax.experimental.pallas import tpu as pltpu
from jax.sharding import PartitionSpec as P

HEADS = 32
HEAD = 80
WIDTH = HEADS * HEAD
ROWS = 256
COARSE = 16
WHOLE = 128
LANES = 128
GROUP = 8
SPAN = GROUP * HEAD
GROUPS = HEADS // GROUP
SEQ = 64
GRP = 4
PICKS = ROWS // COARSE
COARSE_ROWS = SEQ * PICKS
HALF_ROWS = COARSE_ROWS // 2
FAR = ROWS // WHOLE * SEQ // 2
SCALE = HEAD**-0.5
LOG2E = 1.4426950408889634
LOWEST = -1e30
MESH = pl.DeviceIdType.MESH
F32, BF16 = jnp.float32, jnp.bfloat16

NT = (((1,), (1,)), ((), ()))
NN = (((1,), (0,)), ((), ()))


def dot(a, b, dims=NN):
    return lax.dot_general(a, b, dims, preferred_element_type=F32)


def iota(shape, axis):
    return lax.broadcasted_iota(jnp.int32, shape, axis)


def head_of(lane):
    return (lane * 52429) >> 22


def hops(offset):
    return min(offset, 4 - offset)


PLANE = sorted(((dx, dy) for dx in range(4) for dy in range(4)), key=lambda d: -hops(d[0]) - hops(d[1]))


def beyond(p, offset):
    dx, dy = offset
    return (((p >> 3) + dx) & 3) * 8 + ((p + 2 * dy) & 6) + (p & 1)


def eye(n):
    return jnp.where(iota((n, n), 0) == iota((n, n), 1), 1.0, 0.0).astype(BF16)


def window(hh):
    tile, shift = HEAD * hh // LANES, HEAD * hh % LANES
    return tile, shift, 1 if shift + HEAD <= LANES else 2


def in_circle(lane, start, length):
    return ((lane - start) & (LANES - 1)) < length


def group_mask(group):
    shape = (COARSE, SPAN)
    residue = (head_of(iota(shape, 1)) + group * GROUP) & (COARSE - 1)
    return jnp.where(iota(shape, 0) == residue, 1.0, 0.0).astype(BF16)


def pick(x, mask, gather):
    masked = (x.reshape(PICKS, COARSE, SPAN) * mask[None]).reshape(ROWS, SPAN)
    return dot(gather, masked)


def pack_group(group, q, k, v, mask, gather, send, send_pair, q_pick):
    lane = iota((PICKS, LANES), 1)
    qp, kp, vp = (pick(x, mask, gather) for x in (q, k, v))
    q_pick[group] = qp.astype(BF16)
    for hh in range(GROUP):
        tile, shift, tiles = window(hh)

        def circle(x):
            first = x[:, LANES * tile : LANES * (tile + 1)]
            if tiles == 1:
                return first
            return jnp.where(lane >= shift, first, x[:, LANES * (tile + 1) : LANES * (tile + 2)])

        own = in_circle(lane, shift, HEAD)
        vc = circle(vp)
        head, pair = group * GROUP + hh, group * (GROUP // 2) + hh // 2
        first = jnp.where(own, circle(kp), pltpu.roll(vc, HEAD, 1)).astype(BF16)
        rest = pltpu.roll(vc, 32, 1)
        send[head, :, :LANES] = first
        send[head, :, LANES:] = jnp.where(own, circle(qp), rest).astype(BF16)
        if hh % 2 == 0:
            send_pair[pair, :, :LANES] = first
            even = jnp.where(in_circle(lane, shift + HEAD, 32), rest, 0.0)
        else:
            send_pair[pair, :, 2 * LANES :] = first
            send_pair[pair, :, LANES : 2 * LANES] = jnp.where(in_circle(lane, shift + HEAD, 32), rest, even).astype(BF16)


def local_group(group, q, k, v, out):
    unit = eye(LANES)
    half = ROWS // 2
    v_t = jnp.concatenate(
        [dot(unit, v[:, LANES * j : LANES * (j + 1)], NT).astype(BF16) for j in range(SPAN // LANES)], axis=0
    )
    allowed = iota((half, half), 0) <= iota((half, half), 1)
    parts = []
    for hh in range(GROUP):
        tile, shift, tiles = window(hh)
        cols = slice(LANES * tile, LANES * (tile + tiles))
        lane = iota((1, LANES * tiles), 1)
        own = jnp.where((lane >= shift) & (lane < shift + HEAD), 1.0, 0.0).astype(BF16)
        s = dot(k[:, cols], q[:, cols] * own, NT)
        s00 = jnp.where(allowed, s[:half, :half], LOWEST)
        s01 = s[:half, half:]
        s11 = jnp.where(allowed, s[half:, half:], LOWEST)
        top0 = jnp.max(s00, axis=0, keepdims=True)
        top1 = jnp.maximum(jnp.max(s01, axis=0, keepdims=True), jnp.max(s11, axis=0, keepdims=True))
        w00 = jnp.exp2((s00 - top0) * (SCALE * LOG2E))
        w01 = jnp.exp2((s01 - top1) * (SCALE * LOG2E))
        w11 = jnp.exp2((s11 - top1) * (SCALE * LOG2E))
        mass0 = jnp.sum(w00, axis=0, keepdims=True)
        mass1 = jnp.sum(w01, axis=0, keepdims=True) + jnp.sum(w11, axis=0, keepdims=True)
        w = jnp.concatenate(
            [
                jnp.concatenate([w00.astype(BF16), w01.astype(BF16)], axis=1),
                jnp.concatenate([jnp.zeros((half, half), BF16), w11.astype(BF16)], axis=1),
            ],
            axis=0,
        )
        o = dot(v_t[HEAD * hh : HEAD * (hh + 1)], w)
        o = o * (1.0 / jnp.concatenate([mass0, mass1], axis=1))
        parts.append(o.astype(BF16))
    turned = jnp.concatenate(parts, axis=0)
    unit = eye(ROWS)
    for j in range(SPAN // LANES):
        cols = pl.ds(pl.multiple_of(group * SPAN + LANES * j, LANES), LANES)
        out[:, cols] = dot(unit, turned[LANES * j : LANES * (j + 1)], NT).astype(BF16)


def local_picks(group, q_pick, k, v, o_pick, lse_pick):
    shape = (GROUP * PICKS, SPAN)
    own = (iota(shape, 0) >> 4) == head_of(iota(shape, 1))
    q = jnp.concatenate([q_pick] * GROUP, axis=0) * jnp.where(own, 1.0, 0.0).astype(BF16)
    s = dot(q, k, NT)
    row, key = iota(s.shape, 0), iota(s.shape, 1)
    residue = ((row >> 4) + group * GROUP) & (COARSE - 1)
    s = jnp.where(key <= (row & (PICKS - 1)) * COARSE + residue, s, LOWEST)
    top = jnp.max(s, axis=1, keepdims=True)
    w = jnp.exp2((s - top) * (SCALE * LOG2E))
    mass = jnp.sum(w, axis=1, keepdims=True)
    o = dot(w.astype(BF16), v) * (1.0 / mass)
    lse = top * SCALE + jnp.log(mass)
    cols = pl.ds(pl.multiple_of(group * SPAN, LANES), SPAN)
    o_pick[:, cols] = jnp.sum(jnp.where(own, o, 0.0).reshape(GROUP, PICKS, SPAN), axis=0)
    lse_pick[:, cols] = jnp.sum(jnp.where(own, lse, 0.0).reshape(GROUP, PICKS, SPAN), axis=0)


def attend(q, parts, lane, turn):
    scores = [hide(dot(q, keys[:, :LANES], NT)) for keys, hide in parts]
    top = functools.reduce(jnp.maximum, [jnp.max(s, axis=1, keepdims=True) for s in scores])
    weights = [jnp.exp2((s - top) * (SCALE * LOG2E)) for s in scores]
    mass = sum(jnp.sum(w, axis=1, keepdims=True) for w in weights)
    both = sum(dot(w.astype(BF16), keys) for w, (keys, _) in zip(weights, parts))
    o = jnp.where(in_circle(lane, turn + HEAD, 48), both[:, :LANES], pltpu.roll(both[:, LANES:], 48, 1))
    o = o * (1.0 / mass)
    lse = top * SCALE + jnp.log(mass)
    return jnp.where(in_circle(lane, turn + HEAD, HEAD), o, lse)


def place(p, half):
    return (p >> 3) * 16 + half * 8 + (p & 7)


def other_keys(core, other):
    first = other[:, :, :, :, pl.ds(pl.multiple_of(core * 2 * LANES, LANES), LANES)]
    rest = other[:, :, :, :, LANES : 2 * LANES]
    return jnp.concatenate([x.reshape(HALF_ROWS, LANES) for x in (first, rest)], axis=1)


def coarse_blocks(head, half, near, y, back):
    turn = lax.rem(head * HEAD, LANES)
    own = jnp.where(in_circle(iota((1, LANES), 1), turn, HEAD), 1.0, 0.0).astype(BF16)
    step = 128
    below = iota((step, step), 1) <= iota((step, step), 0)
    x = near[...].reshape(HALF_ROWS, 2 * LANES)
    for b in range(HALF_ROWS // step):
        start = b * step

        def last_hidden(s):
            last = jnp.where(below, s[:, start:], LOWEST)
            return last if b == 0 else jnp.concatenate([s[:, :start], last], axis=1)

        parts = [(x[: start + step], last_hidden)]
        if b + half > 0:
            parts.append((y[: start + half * step], lambda s: s))
        q = x[start : start + step, LANES:] * own
        back[start : start + step, :] = attend(q, parts, iota((step, LANES), 1), turn)


def far_rows(head, half, grp, x, far):
    block = 256
    per = block // 8
    chosen = iota((per, block), 1) == iota((per, block), 0) * 8 + head // COARSE
    chosen = jnp.where(chosen, 1.0, 0.0).astype(BF16)
    for b in range(HALF_ROWS // block):
        far[grp, half, per * b : per * (b + 1), :] = dot(chosen, x[block * b : block * (b + 1)]).astype(BF16)


def far_place(r):
    return (r >> 4) * 32 + (r & 15)


def whole_level(head, half, grp, far, back):
    turn = lax.rem(head * HEAD, LANES)
    own = jnp.where(in_circle(iota((1, LANES), 1), turn, HEAD), 1.0, 0.0).astype(BF16)
    keys = far[...].reshape(GRP * 2 * FAR, 2 * LANES)
    q = far[grp, half, :, LANES:] * own

    def hide(s):
        row, col = iota(s.shape, 0), iota(s.shape, 1)
        row = grp * (2 * FAR) + half * 16 + far_place(row)
        col = (col >> 7) * (2 * FAR) + ((col >> 6) & 1) * 16 + far_place(col & (FAR - 1))
        return jnp.where(col <= row, s, LOWEST)

    lane = iota((FAR, LANES), 1)
    mine = attend(q, [(keys, hide)], lane, turn)
    rows = pl.ds(head // COARSE, FAR, stride=8)
    other = back[rows, :]
    result = in_circle(lane, turn + HEAD, HEAD)
    l2 = jnp.max(jnp.where(result, LOWEST * 2, other), axis=1, keepdims=True)
    l3 = jnp.max(jnp.where(result, LOWEST * 2, mine), axis=1, keepdims=True)
    best = jnp.maximum(l2, l3)
    e2, e3 = jnp.exp(l2 - best), jnp.exp(l3 - best)
    total = e2 + e3
    back[rows, :] = jnp.where(result, (e2 * other + e3 * mine) / total, best + jnp.log(total))


def merge_group(group, home, o_pick, lse_pick, out):
    lane = iota((PICKS, LANES), 1)
    tiles_o = [jnp.zeros((PICKS, LANES), F32)] * (SPAN // LANES)
    tiles_l = list(tiles_o)
    for hh in range(GROUP):
        tile, shift, tiles = window(hh)
        m = home[group * GROUP + hh]
        o = pltpu.roll(m, 48, 1)
        at = (shift + 40) % LANES
        lse = jnp.broadcast_to(m[:, at : at + 1], (PICKS, LANES))
        for n in range(tiles):
            here = lane >= shift if n == 0 else lane < shift + HEAD - LANES
            tiles_o[tile + n] = jnp.where(here, o, tiles_o[tile + n])
            tiles_l[tile + n] = jnp.where(here, lse, tiles_l[tile + n])
    for n in range(SPAN // LANES):
        cols = pl.ds(pl.multiple_of(group * SPAN + n * LANES, LANES), LANES)
        l1, l2 = lse_pick[:, cols], tiles_l[n]
        best = jnp.maximum(l1, l2)
        e1, e2 = jnp.exp(l1 - best), jnp.exp(l2 - best)
        merged = (e1 * o_pick[:, cols] + e2 * tiles_o[n]) / (e1 + e2)
        shape = (PICKS, COARSE, LANES)
        residue = head_of(iota((1, COARSE, LANES), 2) + (group * SPAN + n * LANES)) & (COARSE - 1)
        chosen = iota((1, COARSE, LANES), 1) == residue
        rows = jnp.where(chosen, merged.reshape(PICKS, 1, LANES), out[:, cols].reshape(shape).astype(F32))
        out[:, cols] = rows.reshape(ROWS, LANES).astype(BF16)


def kernel(
    q_hbm, k_hbm, v_hbm, out,
    q, k, v, q_pick, o_pick, lse_pick, send, send_pair, near, other, far, back, home,
    in_sem, send_sem, pair_sem, near_sem, other_sem, pass_send, pass_recv, far_send, far_recv, back_send, home_recv,
):
    grp, seq = lax.axis_index("grp"), lax.axis_index("seq")
    half = (seq >> 3) & 1
    head = (seq >> 4) * 8 + (seq & 7)
    core = head & 1
    late = (half == 1) & (head >= HEADS - 8)

    barrier = pltpu.get_barrier_semaphore()

    for h in (1, 0):
        for offset in PLANE:
            for other_core in (1, 0):
                if h or other_core or offset != (0, 0):
                    to = place(beyond(head, offset) ^ other_core, half ^ h)
                    pl.semaphore_signal(barrier, inc=1, device_id=(grp, to), device_id_type=MESH)
        for d in range(1, GRP):
            pl.semaphore_signal(barrier, inc=1, device_id=(grp ^ d, seq ^ (8 * h)), device_id_type=MESH)

    def loads(group):
        cols = pl.ds(pl.multiple_of(group * SPAN, LANES), SPAN)
        return [
            pltpu.make_async_copy(x.at[:, cols], y.at[:, cols], in_sem.at[group, n])
            for n, (x, y) in enumerate(((q_hbm, q), (k_hbm, k), (v_hbm, v)))
        ]

    for group in range(GROUPS):
        for copy in loads(group):
            copy.start()

    gather = jnp.where((iota((PICKS, ROWS), 1) >> 4) == iota((PICKS, ROWS), 0), 1.0, 0.0).astype(BF16)

    def pack(group, _):
        for copy in loads(group):
            copy.wait()
        cols = pl.ds(pl.multiple_of(group * SPAN, LANES), SPAN)
        pack_group(group, q[:, cols], k[:, cols], v[:, cols], group_mask(group), gather, send, send_pair, q_pick)
        return 0

    lax.fori_loop(0, GROUPS, pack, 0)

    pl.semaphore_wait(barrier, SEQ - 1 + 2 * (GRP - 1))

    @pl.when(jnp.logical_not(late))
    def _():
        for offset in PLANE:
            to = beyond(head, offset)
            pltpu.make_async_remote_copy(
                src_ref=send_pair.at[to >> 1], dst_ref=other.at[head >> 3, core, (head >> 1) & 3],
                send_sem=pair_sem, recv_sem=other_sem.at[head >> 3],
                device_id=(grp, place(to, 1 - half)), device_id_type=MESH,
            ).start()

    for offset in PLANE:
        for other_core in (1, 0):
            if other_core or offset != (0, 0):
                to = beyond(head, offset) ^ other_core
                pltpu.make_async_remote_copy(
                    src_ref=send.at[to], dst_ref=near.at[head], send_sem=send_sem, recv_sem=near_sem,
                    device_id=(grp, place(to, half)), device_id_type=MESH,
                ).start()
    pltpu.make_async_copy(send.at[head], near.at[head], near_sem).start()

    def local(group, _):
        cols = pl.ds(pl.multiple_of(group * SPAN, LANES), SPAN)
        local_picks(group, q_pick[group], k[:, cols], v[:, cols], o_pick, lse_pick)
        local_group(group, q[:, cols], k[:, cols], v[:, cols], out)
        return 0

    lax.fori_loop(0, 1, local, 0)

    for g in range(1, GRP):
        @pl.when(grp < g)
        def _():
            far[g] = jnp.zeros((2, FAR, 2 * LANES), BF16)

    @pl.when(half == 0)
    def _():
        other[3] = jnp.zeros((2, 4, PICKS, 3 * LANES), BF16)

    pltpu.make_async_copy(near, near, near_sem).wait()
    far_rows(head, half, grp, near[...].reshape(HALF_ROWS, 2 * LANES), far)

    def far_copy(to, h):
        return pltpu.make_async_remote_copy(
            src_ref=far.at[grp, half], dst_ref=far.at[grp, half],
            send_sem=far_send.at[to, h], recv_sem=far_recv.at[grp, half],
            device_id=(to, place(head, h)), device_id_type=MESH,
        )

    for to in range(1, GRP):
        @pl.when(to > grp)
        def _():
            far_copy(to, 1 - half).start()
            far_copy(to, half).start()

    lax.fori_loop(1, 2, local, 0)

    def pass_on(x):
        part = other.at[x, core, :, :, pl.ds(pl.multiple_of((1 - core) * LANES, LANES), 2 * LANES)]
        return pltpu.make_async_remote_copy(
            src_ref=part, dst_ref=part, send_sem=pass_send.at[x], recv_sem=pass_recv.at[x],
            device_id=(grp, seq ^ 1), device_id_type=MESH,
        )

    for part in range(2):
        @pl.when(half == part)
        def _():
            for x in range(3 + part):
                here = other.at[x, core]
                pltpu.make_async_copy(here, here, other_sem.at[x]).wait()
                pass_on(x).start()
            for x in range(3 + part):
                pass_on(x).wait()
            y = other_keys(core, other)
            far_rows(head, 1 - part, grp, y, far)
            coarse_blocks(head, part, near, y, back)

    for g in range(GRP - 1):
        @pl.when(grp > g)
        def _():
            for h in range(2):
                pltpu.make_async_copy(far.at[g, h], far.at[g, h], far_recv.at[g, h]).wait()

    whole_level(head, half, grp, far, back)

    for offset in PLANE:
        for other_core in (1, 0):
            if other_core or offset != (0, 0):
                to = beyond(head, offset) ^ other_core
                rows = pl.ds(pl.multiple_of(to * PICKS, PICKS), PICKS)
                pltpu.make_async_remote_copy(
                    src_ref=back.at[rows], dst_ref=home.at[head],
                    send_sem=back_send, recv_sem=home_recv.at[head // GROUP],
                    device_id=(grp, place(to, half)), device_id_type=MESH,
                ).start()
    rows = pl.ds(pl.multiple_of(head * PICKS, PICKS), PICKS)
    pltpu.make_async_copy(back.at[rows], home.at[head], home_recv.at[head // GROUP]).start()

    lax.fori_loop(2, GROUPS, local, 0)

    def merge(group, _):
        part = home.at[pl.ds(group * GROUP, GROUP)]
        pltpu.make_async_copy(part, part, home_recv.at[group]).wait()
        merge_group(group, home, o_pick, lse_pick, out)
        return 0

    lax.fori_loop(0, GROUPS, merge, 0)

    most = send.at[pl.ds(0, HEADS - 1)]
    pltpu.make_async_copy(most, most, send_sem).wait()

    @pl.when(jnp.logical_not(late))
    def _():
        pltpu.make_async_copy(send_pair, send_pair, pair_sem).wait()

    for to in range(1, GRP):
        @pl.when(to > grp)
        def _():
            for h in range(2):
                pltpu.make_async_copy(far.at[0, 0], far.at[0, 0], far_send.at[to, h]).wait()
    most = back.at[pl.ds(0, (HEADS - 1) * PICKS)]
    pltpu.make_async_copy(most, most, back_send).wait()


def body(queries, key_matrix, value_matrix):
    return pl.pallas_call(
        kernel,
        out_shape=jax.ShapeDtypeStruct((ROWS, WIDTH), BF16),
        in_specs=[pl.BlockSpec(memory_space=pltpu.HBM)] * 3,
        out_specs=pl.BlockSpec(memory_space=pltpu.VMEM),
        scratch_shapes=[
            pltpu.VMEM((ROWS, WIDTH), BF16),
            pltpu.VMEM((ROWS, WIDTH), BF16),
            pltpu.VMEM((ROWS, WIDTH), BF16),
            pltpu.VMEM((GROUPS, PICKS, SPAN), BF16),
            pltpu.VMEM((PICKS, WIDTH), F32),
            pltpu.VMEM((PICKS, WIDTH), F32),
            pltpu.VMEM((HEADS, PICKS, 2 * LANES), BF16),
            pltpu.VMEM((HEADS // 2, PICKS, 3 * LANES), BF16),
            pltpu.VMEM((HEADS, PICKS, 2 * LANES), BF16),
            pltpu.VMEM((4, 2, 4, PICKS, 3 * LANES), BF16),
            pltpu.VMEM((GRP, 2, FAR, 2 * LANES), BF16),
            pltpu.VMEM((HALF_ROWS, LANES), F32),
            pltpu.VMEM((HEADS, PICKS, LANES), F32),
            pltpu.SemaphoreType.DMA((GROUPS, 3)),
            pltpu.SemaphoreType.DMA,
            pltpu.SemaphoreType.DMA,
            pltpu.SemaphoreType.DMA,
            pltpu.SemaphoreType.DMA((4,)),
            pltpu.SemaphoreType.DMA((4,)),
            pltpu.SemaphoreType.DMA((4,)),
            pltpu.SemaphoreType.DMA((GRP, 2)),
            pltpu.SemaphoreType.DMA((GRP, 2)),
            pltpu.SemaphoreType.DMA,
            pltpu.SemaphoreType.DMA((GROUPS,)),
        ],
        compiler_params=pltpu.CompilerParams(
            collective_id=0, has_side_effects=True, vmem_limit_bytes=48 * 1024 * 1024
        ),
    )(*(pltpu.with_memory_space_constraint(x, pltpu.HBM) for x in (queries, key_matrix, value_matrix)))


def solution(mesh):
    placed = P(("grp", "seq"), None)
    return jax.shard_map(
        body, mesh=mesh, in_specs=(placed,) * 3, out_specs=placed, check_vma=False
    )
```

```python
import functools

import jax
import jax.numpy as jnp
from jax import lax
from jax.experimental import pallas as pl
from jax.experimental.pallas import tpu as pltpu
from jax.sharding import PartitionSpec as P

HEADS = 32
HEAD = 80
WIDTH = HEADS * HEAD
ROWS = 256
COARSE = 16
WHOLE = 128
LANES = 128
GROUP = 8
SPAN = GROUP * HEAD
GROUPS = HEADS // GROUP
SEQ = 64
GRP = 4
PICKS = ROWS // COARSE
COARSE_ROWS = SEQ * PICKS
HALF_ROWS = COARSE_ROWS // 2
FAR = ROWS // WHOLE * SEQ // 2
SCALE = HEAD**-0.5
LOG2E = 1.4426950408889634
LOWEST = -1e30
MESH = pl.DeviceIdType.MESH
F32, BF16 = jnp.float32, jnp.bfloat16

NT = (((1,), (1,)), ((), ()))
NN = (((1,), (0,)), ((), ()))


def dot(a, b, dims=NN):
    return lax.dot_general(a, b, dims, preferred_element_type=F32)


def iota(shape, axis):
    return lax.broadcasted_iota(jnp.int32, shape, axis)


def head_of(lane):
    return (lane * 52429) >> 22


def hops(offset):
    return min(offset, 4 - offset)


PLANE = sorted(((dx, dy) for dx in range(4) for dy in range(4)), key=lambda d: -hops(d[0]) - hops(d[1]))


def beyond(p, offset):
    dx, dy = offset
    return (((p >> 3) + dx) & 3) * 8 + ((p + 2 * dy) & 6) + (p & 1)


def eye(n):
    return jnp.where(iota((n, n), 0) == iota((n, n), 1), 1.0, 0.0).astype(BF16)


def window(hh):
    tile, shift = HEAD * hh // LANES, HEAD * hh % LANES
    return tile, shift, 1 if shift + HEAD <= LANES else 2


def in_circle(lane, start, length):
    return ((lane - start) & (LANES - 1)) < length


def group_mask(group):
    shape = (COARSE, SPAN)
    residue = (head_of(iota(shape, 1)) + group * GROUP) & (COARSE - 1)
    return jnp.where(iota(shape, 0) == residue, 1.0, 0.0).astype(BF16)


def pick(x, mask, gather):
    masked = (x.reshape(PICKS, COARSE, SPAN) * mask[None]).reshape(ROWS, SPAN)
    return dot(gather, masked)


def circle(x, hh):
    tile, shift, tiles = window(hh)
    first = x[:, LANES * tile : LANES * (tile + 1)]
    if tiles == 1:
        return first
    return jnp.where(iota(first.shape, 1) >= shift, first, x[:, LANES * (tile + 1) : LANES * (tile + 2)])


def pack_keys(group, k, v, mask, gather, send, send_pair):
    lane = iota((PICKS, LANES), 1)
    kp, vp = (pick(x, mask, gather) for x in (k, v))
    for hh in range(GROUP):
        shift = window(hh)[1]
        vc = circle(vp, hh)
        head, pair = group * GROUP + hh, group * (GROUP // 2) + hh // 2
        first = jnp.where(in_circle(lane, shift, HEAD), circle(kp, hh), pltpu.roll(vc, HEAD, 1)).astype(BF16)
        rest = pltpu.roll(vc, 32, 1)
        send[head, :, :LANES] = first
        send[head, :, LANES:] = rest.astype(BF16)
        if hh % 2 == 0:
            send_pair[pair, :, :LANES] = first
            even = jnp.where(in_circle(lane, shift + HEAD, 32), rest, 0.0)
        else:
            send_pair[pair, :, 2 * LANES :] = first
            send_pair[pair, :, LANES : 2 * LANES] = jnp.where(in_circle(lane, shift + HEAD, 32), rest, even).astype(BF16)


def pack_queries(group, q, mask, gather, send, q_pick):
    lane = iota((PICKS, LANES), 1)
    qp = pick(q, mask, gather)
    q_pick[group] = qp.astype(BF16)
    for hh in range(GROUP):
        head = group * GROUP + hh
        own = in_circle(lane, window(hh)[1], HEAD)
        rest = send[head, :, LANES:].astype(F32)
        send[head, :, LANES:] = jnp.where(own, circle(qp, hh), rest).astype(BF16)


def local_group(group, q, k, v, out):
    unit = eye(LANES)
    half = ROWS // 2
    v_t = jnp.concatenate(
        [dot(unit, v[:, LANES * j : LANES * (j + 1)], NT).astype(BF16) for j in range(SPAN // LANES)], axis=0
    )
    allowed = iota((half, half), 0) <= iota((half, half), 1)
    parts = []
    for hh in range(GROUP):
        tile, shift, tiles = window(hh)
        cols = slice(LANES * tile, LANES * (tile + tiles))
        lane = iota((1, LANES * tiles), 1)
        own = jnp.where((lane >= shift) & (lane < shift + HEAD), 1.0, 0.0).astype(BF16)
        s = dot(k[:, cols], q[:, cols] * own, NT)
        s00 = jnp.where(allowed, s[:half, :half], LOWEST)
        s01 = s[:half, half:]
        s11 = jnp.where(allowed, s[half:, half:], LOWEST)
        top0 = jnp.max(s00, axis=0, keepdims=True)
        top1 = jnp.maximum(jnp.max(s01, axis=0, keepdims=True), jnp.max(s11, axis=0, keepdims=True))
        w00 = jnp.exp2((s00 - top0) * (SCALE * LOG2E))
        w01 = jnp.exp2((s01 - top1) * (SCALE * LOG2E))
        w11 = jnp.exp2((s11 - top1) * (SCALE * LOG2E))
        mass0 = jnp.sum(w00, axis=0, keepdims=True)
        mass1 = jnp.sum(w01, axis=0, keepdims=True) + jnp.sum(w11, axis=0, keepdims=True)
        w = jnp.concatenate(
            [
                jnp.concatenate([w00.astype(BF16), w01.astype(BF16)], axis=1),
                jnp.concatenate([jnp.zeros((half, half), BF16), w11.astype(BF16)], axis=1),
            ],
            axis=0,
        )
        o = dot(v_t[HEAD * hh : HEAD * (hh + 1)], w)
        o = o * (1.0 / jnp.concatenate([mass0, mass1], axis=1))
        parts.append(o.astype(BF16))
    turned = jnp.concatenate(parts, axis=0)
    unit = eye(ROWS)
    for j in range(SPAN // LANES):
        cols = pl.ds(pl.multiple_of(group * SPAN + LANES * j, LANES), LANES)
        out[:, cols] = dot(unit, turned[LANES * j : LANES * (j + 1)], NT).astype(BF16)


def local_picks(group, q_pick, k, v, o_pick, lse_pick):
    shape = (GROUP * PICKS, SPAN)
    own = (iota(shape, 0) >> 4) == head_of(iota(shape, 1))
    q = jnp.concatenate([q_pick] * GROUP, axis=0) * jnp.where(own, 1.0, 0.0).astype(BF16)
    s = dot(q, k, NT)
    row, key = iota(s.shape, 0), iota(s.shape, 1)
    residue = ((row >> 4) + group * GROUP) & (COARSE - 1)
    s = jnp.where(key <= (row & (PICKS - 1)) * COARSE + residue, s, LOWEST)
    top = jnp.max(s, axis=1, keepdims=True)
    w = jnp.exp2((s - top) * (SCALE * LOG2E))
    mass = jnp.sum(w, axis=1, keepdims=True)
    o = dot(w.astype(BF16), v) * (1.0 / mass)
    lse = top * SCALE + jnp.log(mass)
    cols = pl.ds(pl.multiple_of(group * SPAN, LANES), SPAN)
    o_pick[:, cols] = jnp.sum(jnp.where(own, o, 0.0).reshape(GROUP, PICKS, SPAN), axis=0)
    lse_pick[:, cols] = jnp.sum(jnp.where(own, lse, 0.0).reshape(GROUP, PICKS, SPAN), axis=0)


def attend(q, parts, lane, turn):
    scores = [hide(dot(q, keys[:, :LANES], NT)) for keys, hide in parts]
    top = functools.reduce(jnp.maximum, [jnp.max(s, axis=1, keepdims=True) for s in scores])
    weights = [jnp.exp2((s - top) * (SCALE * LOG2E)) for s in scores]
    mass = sum(jnp.sum(w, axis=1, keepdims=True) for w in weights)
    both = sum(dot(w.astype(BF16), keys) for w, (keys, _) in zip(weights, parts))
    o = jnp.where(in_circle(lane, turn + HEAD, 48), both[:, :LANES], pltpu.roll(both[:, LANES:], 48, 1))
    o = o * (1.0 / mass)
    lse = top * SCALE + jnp.log(mass)
    return jnp.where(in_circle(lane, turn + HEAD, HEAD), o, lse)


def place(p, half):
    return (p >> 3) * 16 + half * 8 + (p & 7)


def other_keys(core, other):
    first = other[:, :, :, :, pl.ds(pl.multiple_of(core * 2 * LANES, LANES), LANES)]
    rest = other[:, :, :, :, LANES : 2 * LANES]
    return jnp.concatenate([x.reshape(HALF_ROWS, LANES) for x in (first, rest)], axis=1)


def coarse_blocks(head, half, near, y, back):
    turn = lax.rem(head * HEAD, LANES)
    own = jnp.where(in_circle(iota((1, LANES), 1), turn, HEAD), 1.0, 0.0).astype(BF16)
    step = 128
    below = iota((step, step), 1) <= iota((step, step), 0)
    x = near[...].reshape(HALF_ROWS, 2 * LANES)
    for b in range(HALF_ROWS // step):
        start = b * step

        def last_hidden(s):
            last = jnp.where(below, s[:, start:], LOWEST)
            return last if b == 0 else jnp.concatenate([s[:, :start], last], axis=1)

        parts = [(x[: start + step], last_hidden)]
        if b + half > 0:
            parts.append((y[: start + half * step], lambda s: s))
        q = x[start : start + step, LANES:] * own
        back[start : start + step, :] = attend(q, parts, iota((step, LANES), 1), turn)


def far_rows(head, half, grp, x, far):
    turn = lax.rem(head * HEAD, LANES)
    block = 256
    per = block // 8
    chosen = iota((per, block), 1) == iota((per, block), 0) * 8 + head // COARSE
    chosen = jnp.where(chosen, 1.0, 0.0).astype(BF16)
    rows = jnp.concatenate([dot(chosen, x[block * b : block * (b + 1)]) for b in range(HALF_ROWS // block)], axis=0)
    far[grp, half, :FAR] = rows[:, :LANES].astype(BF16)
    rest = rows[:, LANES:]
    packed = rest[:PICKS]
    for i in range(1, FAR // PICKS):
        turned = pltpu.roll(rest[PICKS * i : PICKS * (i + 1)], 32 * i, 1)
        packed = jnp.where(in_circle(iota(packed.shape, 1), turn + HEAD + 32 * i, 32), turned, packed)
    far[grp, half, FAR:] = packed.astype(BF16)
    return rest.astype(BF16)


def far_keys(far):
    count = GRP * 2
    first = far[:, :, :FAR].reshape(count * FAR, LANES)
    packed = far[:, :, FAR:].astype(F32).reshape(count * PICKS, LANES)
    turned = [packed] + [pltpu.roll(packed, LANES - 32 * i, 1) for i in range(1, FAR // PICKS)]
    rest = jnp.stack([x.reshape(count, PICKS, LANES) for x in turned], axis=1).reshape(count * FAR, LANES)
    return jnp.concatenate([first, rest.astype(BF16)], axis=1)


def far_place(r):
    return (r >> 4) * 32 + (r & 15)


def whole_level(head, half, grp, far_q, far, back):
    turn = lax.rem(head * HEAD, LANES)
    own = jnp.where(in_circle(iota((1, LANES), 1), turn, HEAD), 1.0, 0.0).astype(BF16)
    keys = far_keys(far)
    q = far_q[...] * own

    def hide(s):
        row, col = iota(s.shape, 0), iota(s.shape, 1)
        row = grp * (2 * FAR) + half * 16 + far_place(row)
        col = (col >> 7) * (2 * FAR) + ((col >> 6) & 1) * 16 + far_place(col & (FAR - 1))
        return jnp.where(col <= row, s, LOWEST)

    lane = iota((FAR, LANES), 1)
    mine = attend(q, [(keys, hide)], lane, turn)
    rows = pl.ds(head // COARSE, FAR, stride=8)
    other = back[rows, :]
    result = in_circle(lane, turn + HEAD, HEAD)
    l2 = jnp.max(jnp.where(result, LOWEST * 2, other), axis=1, keepdims=True)
    l3 = jnp.max(jnp.where(result, LOWEST * 2, mine), axis=1, keepdims=True)
    best = jnp.maximum(l2, l3)
    e2, e3 = jnp.exp(l2 - best), jnp.exp(l3 - best)
    total = e2 + e3
    back[rows, :] = jnp.where(result, (e2 * other + e3 * mine) / total, best + jnp.log(total))


def merge_group(group, home, o_pick, lse_pick, out):
    lane = iota((PICKS, LANES), 1)
    tiles_o = [jnp.zeros((PICKS, LANES), F32)] * (SPAN // LANES)
    tiles_l = list(tiles_o)
    for hh in range(GROUP):
        tile, shift, tiles = window(hh)
        m = home[group * GROUP + hh]
        o = pltpu.roll(m, 48, 1)
        at = (shift + 40) % LANES
        lse = jnp.broadcast_to(m[:, at : at + 1], (PICKS, LANES))
        for n in range(tiles):
            here = lane >= shift if n == 0 else lane < shift + HEAD - LANES
            tiles_o[tile + n] = jnp.where(here, o, tiles_o[tile + n])
            tiles_l[tile + n] = jnp.where(here, lse, tiles_l[tile + n])
    for n in range(SPAN // LANES):
        cols = pl.ds(pl.multiple_of(group * SPAN + n * LANES, LANES), LANES)
        l1, l2 = lse_pick[:, cols], tiles_l[n]
        best = jnp.maximum(l1, l2)
        e1, e2 = jnp.exp(l1 - best), jnp.exp(l2 - best)
        merged = (e1 * o_pick[:, cols] + e2 * tiles_o[n]) / (e1 + e2)
        shape = (PICKS, COARSE, LANES)
        residue = head_of(iota((1, COARSE, LANES), 2) + (group * SPAN + n * LANES)) & (COARSE - 1)
        chosen = iota((1, COARSE, LANES), 1) == residue
        rows = jnp.where(chosen, merged.reshape(PICKS, 1, LANES), out[:, cols].reshape(shape).astype(F32))
        out[:, cols] = rows.reshape(ROWS, LANES).astype(BF16)


def kernel(
    q_hbm, k_hbm, v_hbm, out,
    q, k, v, q_pick, o_pick, lse_pick, send, send_pair, near, other, far_q, far, back, home,
    in_sem, send_sem, pair_sem, near_sem, other_sem, pass_send, pass_recv, far_send, far_recv, back_send, home_recv,
):
    grp, seq = lax.axis_index("grp"), lax.axis_index("seq")
    half = (seq >> 3) & 1
    head = (seq >> 4) * 8 + (seq & 7)
    core = head & 1
    late = (half == 1) & (head >= HEADS - 8)

    barrier = pltpu.get_barrier_semaphore()

    for h in (1, 0):
        for offset in PLANE:
            for other_core in (1, 0):
                if h or other_core or offset != (0, 0):
                    to = place(beyond(head, offset) ^ other_core, half ^ h)
                    pl.semaphore_signal(barrier, inc=1, device_id=(grp, to), device_id_type=MESH)
        for d in range(1, GRP):
            pl.semaphore_signal(barrier, inc=1, device_id=(grp ^ d, seq ^ (8 * h)), device_id_type=MESH)

    def load(group, n):
        cols = pl.ds(pl.multiple_of(group * SPAN, LANES), SPAN)
        x, y = ((q_hbm, q), (k_hbm, k), (v_hbm, v))[n]
        return pltpu.make_async_copy(x.at[:, cols], y.at[:, cols], in_sem.at[group, n])

    for group in range(GROUPS):
        load(group, 1).start()
        load(group, 2).start()
    for group in range(GROUPS):
        load(group, 0).start()

    gather = jnp.where((iota((PICKS, ROWS), 1) >> 4) == iota((PICKS, ROWS), 0), 1.0, 0.0).astype(BF16)

    def pack(group, _):
        load(group, 1).wait()
        load(group, 2).wait()
        cols = pl.ds(pl.multiple_of(group * SPAN, LANES), SPAN)
        pack_keys(group, k[:, cols], v[:, cols], group_mask(group), gather, send, send_pair)
        return 0

    def pack_rest(group, _):
        load(group, 0).wait()
        cols = pl.ds(pl.multiple_of(group * SPAN, LANES), SPAN)
        pack_queries(group, q[:, cols], group_mask(group), gather, send, q_pick)
        return 0

    lax.fori_loop(0, GROUPS, pack, 0)

    def local(group, _):
        cols = pl.ds(pl.multiple_of(group * SPAN, LANES), SPAN)
        local_picks(group, q_pick[group], k[:, cols], v[:, cols], o_pick, lse_pick)
        local_group(group, q[:, cols], k[:, cols], v[:, cols], out)
        return 0

    ahead = jnp.where(half == 0, 2, 0)

    @pl.when(half == 0)
    def _():
        lax.fori_loop(0, GROUPS, pack_rest, 0)
        lax.fori_loop(0, ahead, local, 0)

    pl.semaphore_wait(barrier, SEQ - 1 + 2 * (GRP - 1))

    yields = (half == 1) & (grp == GRP - 1)

    def across():
        for offset in PLANE:
            to = beyond(head, offset)
            pltpu.make_async_remote_copy(
                src_ref=send_pair.at[to >> 1], dst_ref=other.at[head >> 3, core, (head >> 1) & 3],
                send_sem=pair_sem, recv_sem=other_sem.at[head >> 3],
                device_id=(grp, place(to, 1 - half)), device_id_type=MESH,
            ).start()

    @pl.when(jnp.logical_not(late | yields))
    def _():
        across()

    @pl.when(half == 1)
    def _():
        lax.fori_loop(0, GROUPS, pack_rest, 0)

    for offset in PLANE:
        for other_core in (1, 0):
            if other_core or offset != (0, 0):
                to = beyond(head, offset) ^ other_core
                pltpu.make_async_remote_copy(
                    src_ref=send.at[to], dst_ref=near.at[head], send_sem=send_sem, recv_sem=near_sem,
                    device_id=(grp, place(to, half)), device_id_type=MESH,
                ).start()
    pltpu.make_async_copy(send.at[head], near.at[head], near_sem).start()

    @pl.when(jnp.logical_not(late) & yields)
    def _():
        across()

    lax.fori_loop(ahead, jnp.maximum(ahead, 1), local, 0)

    for g in range(1, GRP):
        @pl.when(grp < g)
        def _():
            far[g] = jnp.zeros((2, FAR + PICKS, LANES), BF16)

    @pl.when(half == 0)
    def _():
        other[3] = jnp.zeros((2, 4, PICKS, 3 * LANES), BF16)

    pltpu.make_async_copy(near, near, near_sem).wait()
    far_q[...] = far_rows(head, half, grp, near[...].reshape(HALF_ROWS, 2 * LANES), far)

    def far_copy(to, h):
        return pltpu.make_async_remote_copy(
            src_ref=far.at[grp, half], dst_ref=far.at[grp, half],
            send_sem=far_send.at[to, h], recv_sem=far_recv.at[grp, half],
            device_id=(to, place(head, h)), device_id_type=MESH,
        )

    for to in range(1, GRP):
        @pl.when(to > grp)
        def _():
            far_copy(to, 1 - half).start()
            far_copy(to, half).start()

    lax.fori_loop(jnp.maximum(ahead, 1), jnp.maximum(ahead, 2), local, 0)

    def pass_on(x):
        part = other.at[x, core, :, :, pl.ds(pl.multiple_of((1 - core) * LANES, LANES), 2 * LANES)]
        return pltpu.make_async_remote_copy(
            src_ref=part, dst_ref=part, send_sem=pass_send.at[x], recv_sem=pass_recv.at[x],
            device_id=(grp, seq ^ 1), device_id_type=MESH,
        )

    for part in range(2):
        @pl.when(half == part)
        def _():
            for x in range(3 + part):
                here = other.at[x, core]
                pltpu.make_async_copy(here, here, other_sem.at[x]).wait()
                pass_on(x).start()
            for x in range(3 + part):
                pass_on(x).wait()
            y = other_keys(core, other)
            far_rows(head, 1 - part, grp, y, far)
            coarse_blocks(head, part, near, y, back)

    for g in range(GRP - 1):
        @pl.when(grp > g)
        def _():
            for h in range(2):
                pltpu.make_async_copy(far.at[g, h], far.at[g, h], far_recv.at[g, h]).wait()

    whole_level(head, half, grp, far_q, far, back)

    for offset in PLANE:
        for other_core in (1, 0):
            if other_core or offset != (0, 0):
                to = beyond(head, offset) ^ other_core
                rows = pl.ds(pl.multiple_of(to * PICKS, PICKS), PICKS)
                pltpu.make_async_remote_copy(
                    src_ref=back.at[rows], dst_ref=home.at[head],
                    send_sem=back_send, recv_sem=home_recv.at[head // GROUP],
                    device_id=(grp, place(to, half)), device_id_type=MESH,
                ).start()
    rows = pl.ds(pl.multiple_of(head * PICKS, PICKS), PICKS)
    pltpu.make_async_copy(back.at[rows], home.at[head], home_recv.at[head // GROUP]).start()

    lax.fori_loop(jnp.maximum(ahead, 2), GROUPS, local, 0)

    def merge(group, _):
        part = home.at[pl.ds(group * GROUP, GROUP)]
        pltpu.make_async_copy(part, part, home_recv.at[group]).wait()
        merge_group(group, home, o_pick, lse_pick, out)
        return 0

    lax.fori_loop(0, GROUPS, merge, 0)

    most = send.at[pl.ds(0, HEADS - 1)]
    pltpu.make_async_copy(most, most, send_sem).wait()

    @pl.when(jnp.logical_not(late))
    def _():
        pltpu.make_async_copy(send_pair, send_pair, pair_sem).wait()

    for to in range(1, GRP):
        @pl.when(to > grp)
        def _():
            for h in range(2):
                pltpu.make_async_copy(far.at[0, 0], far.at[0, 0], far_send.at[to, h]).wait()
    most = back.at[pl.ds(0, (HEADS - 1) * PICKS)]
    pltpu.make_async_copy(most, most, back_send).wait()


def body(queries, key_matrix, value_matrix):
    return pl.pallas_call(
        kernel,
        out_shape=jax.ShapeDtypeStruct((ROWS, WIDTH), BF16),
        in_specs=[pl.BlockSpec(memory_space=pltpu.HBM)] * 3,
        out_specs=pl.BlockSpec(memory_space=pltpu.VMEM),
        scratch_shapes=[
            pltpu.VMEM((ROWS, WIDTH), BF16),
            pltpu.VMEM((ROWS, WIDTH), BF16),
            pltpu.VMEM((ROWS, WIDTH), BF16),
            pltpu.VMEM((GROUPS, PICKS, SPAN), BF16),
            pltpu.VMEM((PICKS, WIDTH), F32),
            pltpu.VMEM((PICKS, WIDTH), F32),
            pltpu.VMEM((HEADS, PICKS, 2 * LANES), BF16),
            pltpu.VMEM((HEADS // 2, PICKS, 3 * LANES), BF16),
            pltpu.VMEM((HEADS, PICKS, 2 * LANES), BF16),
            pltpu.VMEM((4, 2, 4, PICKS, 3 * LANES), BF16),
            pltpu.VMEM((FAR, LANES), BF16),
            pltpu.VMEM((GRP, 2, FAR + PICKS, LANES), BF16),
            pltpu.VMEM((HALF_ROWS, LANES), F32),
            pltpu.VMEM((HEADS, PICKS, LANES), F32),
            pltpu.SemaphoreType.DMA((GROUPS, 3)),
            pltpu.SemaphoreType.DMA,
            pltpu.SemaphoreType.DMA,
            pltpu.SemaphoreType.DMA,
            pltpu.SemaphoreType.DMA((4,)),
            pltpu.SemaphoreType.DMA((4,)),
            pltpu.SemaphoreType.DMA((4,)),
            pltpu.SemaphoreType.DMA((GRP, 2)),
            pltpu.SemaphoreType.DMA((GRP, 2)),
            pltpu.SemaphoreType.DMA,
            pltpu.SemaphoreType.DMA((GROUPS,)),
        ],
        compiler_params=pltpu.CompilerParams(
            collective_id=0, has_side_effects=True, vmem_limit_bytes=48 * 1024 * 1024
        ),
    )(*(pltpu.with_memory_space_constraint(x, pltpu.HBM) for x in (queries, key_matrix, value_matrix)))


def solution(mesh):
    placed = P(("grp", "seq"), None)
    return jax.shard_map(
        body, mesh=mesh, in_specs=(placed,) * 3, out_specs=placed, check_vma=False
    )
```

```python
import functools

import jax
import jax.numpy as jnp
from jax import lax
from jax.experimental import pallas as pl
from jax.experimental.pallas import tpu as pltpu
from jax.sharding import PartitionSpec as P

HEADS = 32
HEAD = 80
WIDTH = HEADS * HEAD
ROWS = 256
COARSE = 16
WHOLE = 128
LANES = 128
GROUP = 8
SPAN = GROUP * HEAD
GROUPS = HEADS // GROUP
SEQ = 64
GRP = 4
PICKS = ROWS // COARSE
COARSE_ROWS = SEQ * PICKS
HALF_ROWS = COARSE_ROWS // 2
FAR = ROWS // WHOLE * SEQ // 2
SCALE = HEAD**-0.5
LOG2E = 1.4426950408889634
LOWEST = -1e30
MESH = pl.DeviceIdType.MESH
F32, BF16 = jnp.float32, jnp.bfloat16

NT = (((1,), (1,)), ((), ()))
NN = (((1,), (0,)), ((), ()))


def dot(a, b, dims=NN):
    return lax.dot_general(a, b, dims, preferred_element_type=F32)


def iota(shape, axis):
    return lax.broadcasted_iota(jnp.int32, shape, axis)


def head_of(lane):
    return (lane * 52429) >> 22


def hops(offset):
    return min(offset, 4 - offset)


PLANE = sorted(((dx, dy) for dx in range(4) for dy in range(4)), key=lambda d: -hops(d[0]) - hops(d[1]))


def beyond(p, offset):
    dx, dy = offset
    return (((p >> 3) + dx) & 3) * 8 + ((p + 2 * dy) & 6) + (p & 1)


def eye(n):
    return jnp.where(iota((n, n), 0) == iota((n, n), 1), 1.0, 0.0).astype(BF16)


def window(hh):
    tile, shift = HEAD * hh // LANES, HEAD * hh % LANES
    return tile, shift, 1 if shift + HEAD <= LANES else 2


def in_circle(lane, start, length):
    return ((lane - start) & (LANES - 1)) < length


def group_mask(group):
    shape = (COARSE, SPAN)
    residue = (head_of(iota(shape, 1)) + group * GROUP) & (COARSE - 1)
    return jnp.where(iota(shape, 0) == residue, 1.0, 0.0).astype(BF16)


def pick(x, mask, gather):
    masked = (x.reshape(PICKS, COARSE, SPAN) * mask[None]).reshape(ROWS, SPAN)
    return dot(gather, masked)


def circle(x, hh):
    tile, shift, tiles = window(hh)
    first = x[:, LANES * tile : LANES * (tile + 1)]
    if tiles == 1:
        return first
    return jnp.where(iota(first.shape, 1) >= shift, first, x[:, LANES * (tile + 1) : LANES * (tile + 2)])


def pack_keys(group, k, v, mask, gather, send, send_pair):
    lane = iota((PICKS, LANES), 1)
    kp, vp = (pick(x, mask, gather) for x in (k, v))
    for hh in range(GROUP):
        shift = window(hh)[1]
        vc = circle(vp, hh)
        head, pair = group * GROUP + hh, group * (GROUP // 2) + hh // 2
        first = jnp.where(in_circle(lane, shift, HEAD), circle(kp, hh), pltpu.roll(vc, HEAD, 1)).astype(BF16)
        rest = pltpu.roll(vc, 32, 1)
        send[head, :, :LANES] = first
        send[head, :, LANES:] = rest.astype(BF16)
        if hh % 2 == 0:
            send_pair[pair, :, :LANES] = first
            even = jnp.where(in_circle(lane, shift + HEAD, 32), rest, 0.0)
        else:
            send_pair[pair, :, 2 * LANES :] = first
            send_pair[pair, :, LANES : 2 * LANES] = jnp.where(in_circle(lane, shift + HEAD, 32), rest, even).astype(BF16)


def pack_queries(group, q, mask, gather, send, q_pick):
    lane = iota((PICKS, LANES), 1)
    qp = pick(q, mask, gather)
    q_pick[group] = qp.astype(BF16)
    for hh in range(GROUP):
        head = group * GROUP + hh
        own = in_circle(lane, window(hh)[1], HEAD)
        rest = send[head, :, LANES:].astype(F32)
        send[head, :, LANES:] = jnp.where(own, circle(qp, hh), rest).astype(BF16)


def local_group(group, q, k, v, out):
    unit = eye(LANES)
    half = ROWS // 2
    v_t = jnp.concatenate(
        [dot(unit, v[:, LANES * j : LANES * (j + 1)], NT).astype(BF16) for j in range(SPAN // LANES)], axis=0
    )
    allowed = iota((half, half), 0) <= iota((half, half), 1)
    parts = []
    for hh in range(GROUP):
        tile, shift, tiles = window(hh)
        cols = slice(LANES * tile, LANES * (tile + tiles))
        lane = iota((1, LANES * tiles), 1)
        own = jnp.where((lane >= shift) & (lane < shift + HEAD), 1.0, 0.0).astype(BF16)
        s = dot(k[:, cols], q[:, cols] * own, NT)
        s00 = jnp.where(allowed, s[:half, :half], LOWEST)
        s01 = s[:half, half:]
        s11 = jnp.where(allowed, s[half:, half:], LOWEST)
        top0 = jnp.max(s00, axis=0, keepdims=True)
        top1 = jnp.maximum(jnp.max(s01, axis=0, keepdims=True), jnp.max(s11, axis=0, keepdims=True))
        w00 = jnp.exp2((s00 - top0) * (SCALE * LOG2E))
        w01 = jnp.exp2((s01 - top1) * (SCALE * LOG2E))
        w11 = jnp.exp2((s11 - top1) * (SCALE * LOG2E))
        mass0 = jnp.sum(w00, axis=0, keepdims=True)
        mass1 = jnp.sum(w01, axis=0, keepdims=True) + jnp.sum(w11, axis=0, keepdims=True)
        w = jnp.concatenate(
            [
                jnp.concatenate([w00.astype(BF16), w01.astype(BF16)], axis=1),
                jnp.concatenate([jnp.zeros((half, half), BF16), w11.astype(BF16)], axis=1),
            ],
            axis=0,
        )
        o = dot(v_t[HEAD * hh : HEAD * (hh + 1)], w)
        o = o * (1.0 / jnp.concatenate([mass0, mass1], axis=1))
        parts.append(o.astype(BF16))
    turned = jnp.concatenate(parts, axis=0)
    unit = eye(ROWS)
    for j in range(SPAN // LANES):
        cols = pl.ds(pl.multiple_of(group * SPAN + LANES * j, LANES), LANES)
        out[:, cols] = dot(unit, turned[LANES * j : LANES * (j + 1)], NT).astype(BF16)


def local_picks(group, q_pick, k, v, o_pick, lse_pick):
    shape = (GROUP * PICKS, SPAN)
    own = (iota(shape, 0) >> 4) == head_of(iota(shape, 1))
    q = jnp.concatenate([q_pick] * GROUP, axis=0) * jnp.where(own, 1.0, 0.0).astype(BF16)
    s = dot(q, k, NT)
    row, key = iota(s.shape, 0), iota(s.shape, 1)
    residue = ((row >> 4) + group * GROUP) & (COARSE - 1)
    s = jnp.where(key <= (row & (PICKS - 1)) * COARSE + residue, s, LOWEST)
    top = jnp.max(s, axis=1, keepdims=True)
    w = jnp.exp2((s - top) * (SCALE * LOG2E))
    mass = jnp.sum(w, axis=1, keepdims=True)
    o = dot(w.astype(BF16), v) * (1.0 / mass)
    lse = top * SCALE + jnp.log(mass)
    cols = pl.ds(pl.multiple_of(group * SPAN, LANES), SPAN)
    o_pick[:, cols] = jnp.sum(jnp.where(own, o, 0.0).reshape(GROUP, PICKS, SPAN), axis=0)
    lse_pick[:, cols] = jnp.sum(jnp.where(own, lse, 0.0).reshape(GROUP, PICKS, SPAN), axis=0)


def attend(q, parts, lane, turn):
    scores, tops = [], []
    for keys, known in parts:
        if callable(known):
            s = known(dot(q, keys[:, :LANES], NT))
            known = s, jnp.max(s, axis=1, keepdims=True)
        scores.append(known[0])
        tops.append(known[1])
    top = functools.reduce(jnp.maximum, tops)
    weights = [jnp.exp2((s - top) * (SCALE * LOG2E)) for s in scores]
    mass = sum(jnp.sum(w, axis=1, keepdims=True) for w in weights)
    both = sum(dot(w.astype(BF16), keys) for w, (keys, _) in zip(weights, parts))
    o = jnp.where(in_circle(lane, turn + HEAD, 48), both[:, :LANES], pltpu.roll(both[:, LANES:], 48, 1))
    o = o * (1.0 / mass)
    lse = top * SCALE + jnp.log(mass)
    return jnp.where(in_circle(lane, turn + HEAD, HEAD), o, lse)


def place(p, half):
    return (p >> 3) * 16 + half * 8 + (p & 7)


def other_keys(core, other):
    first = other[:, :, :, :, pl.ds(pl.multiple_of(core * 2 * LANES, LANES), LANES)]
    rest = other[:, :, :, :, LANES : 2 * LANES]
    return jnp.concatenate([x.reshape(HALF_ROWS, LANES) for x in (first, rest)], axis=1)


STEP = 128


def near_scores(head, near, scores, tops):
    turn = lax.rem(head * HEAD, LANES)
    own = jnp.where(in_circle(iota((1, LANES), 1), turn, HEAD), 1.0, 0.0).astype(BF16)
    below = iota((STEP, STEP), 1) <= iota((STEP, STEP), 0)
    x = near[...].reshape(HALF_ROWS, 2 * LANES)
    for start in range(0, HALF_ROWS, STEP):
        end = start + STEP
        s = dot(x[start:end, LANES:] * own, x[:end, :LANES], NT)
        last = jnp.where(below, s[:, start:], LOWEST)
        s = last if start == 0 else jnp.concatenate([s[:, :start], last], axis=1)
        scores[start:end, :end] = s
        tops[start:end, :] = jnp.broadcast_to(jnp.max(s, axis=1, keepdims=True), (STEP, LANES))


def coarse_blocks(head, half, near, y, scores, tops, back):
    turn = lax.rem(head * HEAD, LANES)
    own = jnp.where(in_circle(iota((1, LANES), 1), turn, HEAD), 1.0, 0.0).astype(BF16)
    x = near[...].reshape(HALF_ROWS, 2 * LANES)
    for b in range(HALF_ROWS // STEP):
        start, end = b * STEP, (b + 1) * STEP
        parts = [(x[:end], (scores[start:end, :end], tops[start:end, :1]))]
        if b + half > 0:
            parts.append((y[: start + half * STEP], lambda s: s))
        q = x[start:end, LANES:] * own
        back[start:end, :] = attend(q, parts, iota((STEP, LANES), 1), turn)


def far_rows(head, half, grp, x, far):
    turn = lax.rem(head * HEAD, LANES)
    block = 256
    per = block // 8
    chosen = iota((per, block), 1) == iota((per, block), 0) * 8 + head // COARSE
    chosen = jnp.where(chosen, 1.0, 0.0).astype(BF16)
    rows = jnp.concatenate([dot(chosen, x[block * b : block * (b + 1)]) for b in range(HALF_ROWS // block)], axis=0)
    far[grp, half, :FAR] = rows[:, :LANES].astype(BF16)
    rest = rows[:, LANES:]
    packed = rest[:PICKS]
    for i in range(1, FAR // PICKS):
        turned = pltpu.roll(rest[PICKS * i : PICKS * (i + 1)], 32 * i, 1)
        packed = jnp.where(in_circle(iota(packed.shape, 1), turn + HEAD + 32 * i, 32), turned, packed)
    far[grp, half, FAR:] = packed.astype(BF16)
    return rest.astype(BF16)


def far_keys(far):
    count = GRP * 2
    first = far[:, :, :FAR].reshape(count * FAR, LANES)
    packed = far[:, :, FAR:].astype(F32).reshape(count * PICKS, LANES)
    turned = [packed] + [pltpu.roll(packed, LANES - 32 * i, 1) for i in range(1, FAR // PICKS)]
    rest = jnp.stack([x.reshape(count, PICKS, LANES) for x in turned], axis=1).reshape(count * FAR, LANES)
    return jnp.concatenate([first, rest.astype(BF16)], axis=1)


def far_place(r):
    return (r >> 4) * 32 + (r & 15)


def whole_level(head, half, grp, far_q, far, back):
    turn = lax.rem(head * HEAD, LANES)
    own = jnp.where(in_circle(iota((1, LANES), 1), turn, HEAD), 1.0, 0.0).astype(BF16)
    keys = far_keys(far)
    q = far_q[...] * own

    def hide(s):
        row, col = iota(s.shape, 0), iota(s.shape, 1)
        row = grp * (2 * FAR) + half * 16 + far_place(row)
        col = (col >> 7) * (2 * FAR) + ((col >> 6) & 1) * 16 + far_place(col & (FAR - 1))
        return jnp.where(col <= row, s, LOWEST)

    lane = iota((FAR, LANES), 1)
    mine = attend(q, [(keys, hide)], lane, turn)
    rows = pl.ds(head // COARSE, FAR, stride=8)
    other = back[rows, :]
    result = in_circle(lane, turn + HEAD, HEAD)
    l2 = jnp.max(jnp.where(result, LOWEST * 2, other), axis=1, keepdims=True)
    l3 = jnp.max(jnp.where(result, LOWEST * 2, mine), axis=1, keepdims=True)
    best = jnp.maximum(l2, l3)
    e2, e3 = jnp.exp(l2 - best), jnp.exp(l3 - best)
    total = e2 + e3
    back[rows, :] = jnp.where(result, (e2 * other + e3 * mine) / total, best + jnp.log(total))


def merge_group(group, home, o_pick, lse_pick, out):
    lane = iota((PICKS, LANES), 1)
    tiles_o = [jnp.zeros((PICKS, LANES), F32)] * (SPAN // LANES)
    tiles_l = list(tiles_o)
    for hh in range(GROUP):
        tile, shift, tiles = window(hh)
        m = home[group * GROUP + hh]
        o = pltpu.roll(m, 48, 1)
        at = (shift + 40) % LANES
        lse = jnp.broadcast_to(m[:, at : at + 1], (PICKS, LANES))
        for n in range(tiles):
            here = lane >= shift if n == 0 else lane < shift + HEAD - LANES
            tiles_o[tile + n] = jnp.where(here, o, tiles_o[tile + n])
            tiles_l[tile + n] = jnp.where(here, lse, tiles_l[tile + n])
    for n in range(SPAN // LANES):
        cols = pl.ds(pl.multiple_of(group * SPAN + n * LANES, LANES), LANES)
        l1, l2 = lse_pick[:, cols], tiles_l[n]
        best = jnp.maximum(l1, l2)
        e1, e2 = jnp.exp(l1 - best), jnp.exp(l2 - best)
        merged = (e1 * o_pick[:, cols] + e2 * tiles_o[n]) / (e1 + e2)
        shape = (PICKS, COARSE, LANES)
        residue = head_of(iota((1, COARSE, LANES), 2) + (group * SPAN + n * LANES)) & (COARSE - 1)
        chosen = iota((1, COARSE, LANES), 1) == residue
        rows = jnp.where(chosen, merged.reshape(PICKS, 1, LANES), out[:, cols].reshape(shape).astype(F32))
        out[:, cols] = rows.reshape(ROWS, LANES).astype(BF16)


def kernel(
    q_hbm, k_hbm, v_hbm, out,
    q, k, v, q_pick, o_pick, lse_pick, send, send_pair, near, other, far_q, far, scores, tops, back, home,
    in_sem, send_sem, pair_sem, near_sem, other_sem, pass_send, pass_recv, far_send, far_recv, back_send, home_recv,
):
    grp, seq = lax.axis_index("grp"), lax.axis_index("seq")
    half = (seq >> 3) & 1
    head = (seq >> 4) * 8 + (seq & 7)
    core = head & 1
    late = (half == 1) & (head >= HEADS - 8)

    barrier = pltpu.get_barrier_semaphore()

    for h in (1, 0):
        for offset in PLANE:
            for other_core in (1, 0):
                if h or other_core or offset != (0, 0):
                    to = place(beyond(head, offset) ^ other_core, half ^ h)
                    pl.semaphore_signal(barrier, inc=1, device_id=(grp, to), device_id_type=MESH)
        for d in range(1, GRP):
            pl.semaphore_signal(barrier, inc=1, device_id=(grp ^ d, seq ^ (8 * h)), device_id_type=MESH)

    def load(group, n):
        cols = pl.ds(pl.multiple_of(group * SPAN, LANES), SPAN)
        x, y = ((q_hbm, q), (k_hbm, k), (v_hbm, v))[n]
        return pltpu.make_async_copy(x.at[:, cols], y.at[:, cols], in_sem.at[group, n])

    for group in range(GROUPS):
        load(group, 1).start()
        load(group, 2).start()
    for group in range(GROUPS):
        load(group, 0).start()

    gather = jnp.where((iota((PICKS, ROWS), 1) >> 4) == iota((PICKS, ROWS), 0), 1.0, 0.0).astype(BF16)

    def pack(group, _):
        load(group, 1).wait()
        load(group, 2).wait()
        cols = pl.ds(pl.multiple_of(group * SPAN, LANES), SPAN)
        pack_keys(group, k[:, cols], v[:, cols], group_mask(group), gather, send, send_pair)
        return 0

    def pack_rest(group, _):
        load(group, 0).wait()
        cols = pl.ds(pl.multiple_of(group * SPAN, LANES), SPAN)
        pack_queries(group, q[:, cols], group_mask(group), gather, send, q_pick)
        return 0

    lax.fori_loop(0, GROUPS, pack, 0)

    def local(group, _):
        cols = pl.ds(pl.multiple_of(group * SPAN, LANES), SPAN)
        local_picks(group, q_pick[group], k[:, cols], v[:, cols], o_pick, lse_pick)
        local_group(group, q[:, cols], k[:, cols], v[:, cols], out)
        return 0

    ahead = jnp.where(half == 0, 2, 0)

    @pl.when(half == 0)
    def _():
        lax.fori_loop(0, GROUPS, pack_rest, 0)
        lax.fori_loop(0, ahead, local, 0)

    pl.semaphore_wait(barrier, SEQ - 1 + 2 * (GRP - 1))

    yields = (half == 1) & (grp == GRP - 1)

    def across():
        for offset in PLANE:
            to = beyond(head, offset)
            pltpu.make_async_remote_copy(
                src_ref=send_pair.at[to >> 1], dst_ref=other.at[head >> 3, core, (head >> 1) & 3],
                send_sem=pair_sem, recv_sem=other_sem.at[head >> 3],
                device_id=(grp, place(to, 1 - half)), device_id_type=MESH,
            ).start()

    @pl.when(jnp.logical_not(late | yields))
    def _():
        across()

    @pl.when(half == 1)
    def _():
        lax.fori_loop(0, GROUPS, pack_rest, 0)

    for offset in PLANE:
        for other_core in (1, 0):
            if other_core or offset != (0, 0):
                to = beyond(head, offset) ^ other_core
                pltpu.make_async_remote_copy(
                    src_ref=send.at[to], dst_ref=near.at[head], send_sem=send_sem, recv_sem=near_sem,
                    device_id=(grp, place(to, half)), device_id_type=MESH,
                ).start()
    pltpu.make_async_copy(send.at[head], near.at[head], near_sem).start()

    @pl.when(jnp.logical_not(late) & yields)
    def _():
        across()

    lax.fori_loop(ahead, jnp.maximum(ahead, 1), local, 0)

    for g in range(1, GRP):
        @pl.when(grp < g)
        def _():
            far[g] = jnp.zeros((2, FAR + PICKS, LANES), BF16)

    @pl.when(half == 0)
    def _():
        other[3] = jnp.zeros((2, 4, PICKS, 3 * LANES), BF16)

    pltpu.make_async_copy(near, near, near_sem).wait()
    far_q[...] = far_rows(head, half, grp, near[...].reshape(HALF_ROWS, 2 * LANES), far)

    def far_copy(to, h):
        return pltpu.make_async_remote_copy(
            src_ref=far.at[grp, half], dst_ref=far.at[grp, half],
            send_sem=far_send.at[to, h], recv_sem=far_recv.at[grp, half],
            device_id=(to, place(head, h)), device_id_type=MESH,
        )

    for to in range(1, GRP):
        @pl.when(to > grp)
        def _():
            far_copy(to, 1 - half).start()
            far_copy(to, half).start()

    near_scores(head, near, scores, tops)
    lax.fori_loop(jnp.maximum(ahead, 1), jnp.maximum(ahead, 2), local, 0)

    def pass_on(x):
        part = other.at[x, core, :, :, pl.ds(pl.multiple_of((1 - core) * LANES, LANES), 2 * LANES)]
        return pltpu.make_async_remote_copy(
            src_ref=part, dst_ref=part, send_sem=pass_send.at[x], recv_sem=pass_recv.at[x],
            device_id=(grp, seq ^ 1), device_id_type=MESH,
        )

    for part in range(2):
        @pl.when(half == part)
        def _():
            for x in range(3 + part):
                here = other.at[x, core]
                pltpu.make_async_copy(here, here, other_sem.at[x]).wait()
                pass_on(x).start()
            for x in range(3 + part):
                pass_on(x).wait()
            y = other_keys(core, other)
            far_rows(head, 1 - part, grp, y, far)
            coarse_blocks(head, part, near, y, scores, tops, back)

    for g in range(GRP - 1):
        @pl.when(grp > g)
        def _():
            for h in range(2):
                pltpu.make_async_copy(far.at[g, h], far.at[g, h], far_recv.at[g, h]).wait()

    whole_level(head, half, grp, far_q, far, back)

    for offset in PLANE:
        for other_core in (1, 0):
            if other_core or offset != (0, 0):
                to = beyond(head, offset) ^ other_core
                rows = pl.ds(pl.multiple_of(to * PICKS, PICKS), PICKS)
                pltpu.make_async_remote_copy(
                    src_ref=back.at[rows], dst_ref=home.at[head],
                    send_sem=back_send, recv_sem=home_recv.at[head // GROUP],
                    device_id=(grp, place(to, half)), device_id_type=MESH,
                ).start()
    rows = pl.ds(pl.multiple_of(head * PICKS, PICKS), PICKS)
    pltpu.make_async_copy(back.at[rows], home.at[head], home_recv.at[head // GROUP]).start()

    lax.fori_loop(jnp.maximum(ahead, 2), GROUPS, local, 0)

    def merge(group, _):
        part = home.at[pl.ds(group * GROUP, GROUP)]
        pltpu.make_async_copy(part, part, home_recv.at[group]).wait()
        merge_group(group, home, o_pick, lse_pick, out)
        return 0

    lax.fori_loop(0, GROUPS, merge, 0)

    most = send.at[pl.ds(0, HEADS - 1)]
    pltpu.make_async_copy(most, most, send_sem).wait()

    @pl.when(jnp.logical_not(late))
    def _():
        pltpu.make_async_copy(send_pair, send_pair, pair_sem).wait()

    for to in range(1, GRP):
        @pl.when(to > grp)
        def _():
            for h in range(2):
                pltpu.make_async_copy(far.at[0, 0], far.at[0, 0], far_send.at[to, h]).wait()
    most = back.at[pl.ds(0, (HEADS - 1) * PICKS)]
    pltpu.make_async_copy(most, most, back_send).wait()


def body(queries, key_matrix, value_matrix):
    return pl.pallas_call(
        kernel,
        out_shape=jax.ShapeDtypeStruct((ROWS, WIDTH), BF16),
        in_specs=[pl.BlockSpec(memory_space=pltpu.HBM)] * 3,
        out_specs=pl.BlockSpec(memory_space=pltpu.VMEM),
        scratch_shapes=[
            pltpu.VMEM((ROWS, WIDTH), BF16),
            pltpu.VMEM((ROWS, WIDTH), BF16),
            pltpu.VMEM((ROWS, WIDTH), BF16),
            pltpu.VMEM((GROUPS, PICKS, SPAN), BF16),
            pltpu.VMEM((PICKS, WIDTH), F32),
            pltpu.VMEM((PICKS, WIDTH), F32),
            pltpu.VMEM((HEADS, PICKS, 2 * LANES), BF16),
            pltpu.VMEM((HEADS // 2, PICKS, 3 * LANES), BF16),
            pltpu.VMEM((HEADS, PICKS, 2 * LANES), BF16),
            pltpu.VMEM((4, 2, 4, PICKS, 3 * LANES), BF16),
            pltpu.VMEM((FAR, LANES), BF16),
            pltpu.VMEM((GRP, 2, FAR + PICKS, LANES), BF16),
            pltpu.VMEM((HALF_ROWS, HALF_ROWS), F32),
            pltpu.VMEM((HALF_ROWS, LANES), F32),
            pltpu.VMEM((HALF_ROWS, LANES), F32),
            pltpu.VMEM((HEADS, PICKS, LANES), F32),
            pltpu.SemaphoreType.DMA((GROUPS, 3)),
            pltpu.SemaphoreType.DMA,
            pltpu.SemaphoreType.DMA,
            pltpu.SemaphoreType.DMA,
            pltpu.SemaphoreType.DMA((4,)),
            pltpu.SemaphoreType.DMA((4,)),
            pltpu.SemaphoreType.DMA((4,)),
            pltpu.SemaphoreType.DMA((GRP, 2)),
            pltpu.SemaphoreType.DMA((GRP, 2)),
            pltpu.SemaphoreType.DMA,
            pltpu.SemaphoreType.DMA((GROUPS,)),
        ],
        compiler_params=pltpu.CompilerParams(
            collective_id=0, has_side_effects=True, vmem_limit_bytes=48 * 1024 * 1024
        ),
    )(*(pltpu.with_memory_space_constraint(x, pltpu.HBM) for x in (queries, key_matrix, value_matrix)))


def solution(mesh):
    placed = P(("grp", "seq"), None)
    return jax.shard_map(
        body, mesh=mesh, in_specs=(placed,) * 3, out_specs=placed, check_vma=False
    )
```

```python
import functools

import jax
import jax.numpy as jnp
from jax import lax
from jax.experimental import pallas as pl
from jax.experimental.pallas import tpu as pltpu
from jax.sharding import PartitionSpec as P

HEADS = 32
HEAD = 80
WIDTH = HEADS * HEAD
ROWS = 256
COARSE = 16
WHOLE = 128
LANES = 128
GROUP = 8
SPAN = GROUP * HEAD
GROUPS = HEADS // GROUP
SEQ = 64
GRP = 4
PICKS = ROWS // COARSE
COARSE_ROWS = SEQ * PICKS
HALF_ROWS = COARSE_ROWS // 2
FAR = ROWS // WHOLE * SEQ // 2
SCALE = HEAD**-0.5
LOG2E = 1.4426950408889634
LOWEST = -1e30
MESH = pl.DeviceIdType.MESH
F32, BF16 = jnp.float32, jnp.bfloat16

NT = (((1,), (1,)), ((), ()))
NN = (((1,), (0,)), ((), ()))


def dot(a, b, dims=NN):
    return lax.dot_general(a, b, dims, preferred_element_type=F32)


def iota(shape, axis):
    return lax.broadcasted_iota(jnp.int32, shape, axis)


def head_of(lane):
    return (lane * 52429) >> 22


def hops(offset):
    return min(offset, 4 - offset)


PLANE = sorted(((dx, dy) for dx in range(4) for dy in range(4)), key=lambda d: -hops(d[0]) - hops(d[1]))


def beyond(p, offset):
    dx, dy = offset
    return (((p >> 3) + dx) & 3) * 8 + ((p + 2 * dy) & 6) + (p & 1)


def eye(n):
    return jnp.where(iota((n, n), 0) == iota((n, n), 1), 1.0, 0.0).astype(BF16)


def window(hh):
    tile, shift = HEAD * hh // LANES, HEAD * hh % LANES
    return tile, shift, 1 if shift + HEAD <= LANES else 2


def in_circle(lane, start, length):
    return ((lane - start) & (LANES - 1)) < length


def group_mask(group):
    shape = (COARSE, SPAN)
    residue = (head_of(iota(shape, 1)) + group * GROUP) & (COARSE - 1)
    return jnp.where(iota(shape, 0) == residue, 1.0, 0.0).astype(BF16)


def pick(x, mask, gather):
    masked = (x.reshape(PICKS, COARSE, SPAN) * mask[None]).reshape(ROWS, SPAN)
    return dot(gather, masked)


def circle(x, hh):
    tile, shift, tiles = window(hh)
    first = x[:, LANES * tile : LANES * (tile + 1)]
    if tiles == 1:
        return first
    return jnp.where(iota(first.shape, 1) >= shift, first, x[:, LANES * (tile + 1) : LANES * (tile + 2)])


def pack_keys(group, k, v, mask, gather, send, send_pair):
    lane = iota((PICKS, LANES), 1)
    kp, vp = (pick(x, mask, gather) for x in (k, v))
    for hh in range(GROUP):
        shift = window(hh)[1]
        vc = circle(vp, hh)
        head, pair = group * GROUP + hh, group * (GROUP // 2) + hh // 2
        first = jnp.where(in_circle(lane, shift, HEAD), circle(kp, hh), pltpu.roll(vc, HEAD, 1)).astype(BF16)
        rest = pltpu.roll(vc, 32, 1)
        send[head, :, :LANES] = first
        send[head, :, LANES:] = rest.astype(BF16)
        if hh % 2 == 0:
            send_pair[pair, :, :LANES] = first
            even = jnp.where(in_circle(lane, shift + HEAD, 32), rest, 0.0)
        else:
            send_pair[pair, :, 2 * LANES :] = first
            send_pair[pair, :, LANES : 2 * LANES] = jnp.where(in_circle(lane, shift + HEAD, 32), rest, even).astype(BF16)


def pack_queries(group, q, mask, gather, send, q_pick):
    lane = iota((PICKS, LANES), 1)
    qp = pick(q, mask, gather)
    q_pick[group] = qp.astype(BF16)
    for hh in range(GROUP):
        head = group * GROUP + hh
        own = in_circle(lane, window(hh)[1], HEAD)
        rest = send[head, :, LANES:].astype(F32)
        send[head, :, LANES:] = jnp.where(own, circle(qp, hh), rest).astype(BF16)


def local_group(group, q, k, v, out):
    unit = eye(LANES)
    half = ROWS // 2
    v_t = jnp.concatenate(
        [dot(unit, v[:, LANES * j : LANES * (j + 1)], NT).astype(BF16) for j in range(SPAN // LANES)], axis=0
    )
    allowed = iota((half, half), 0) <= iota((half, half), 1)
    parts = []
    for hh in range(GROUP):
        tile, shift, tiles = window(hh)
        cols = slice(LANES * tile, LANES * (tile + tiles))
        lane = iota((1, LANES * tiles), 1)
        own = jnp.where((lane >= shift) & (lane < shift + HEAD), 1.0, 0.0).astype(BF16)
        s = dot(k[:, cols], q[:, cols] * own, NT)
        s00 = jnp.where(allowed, s[:half, :half], LOWEST)
        s01 = s[:half, half:]
        s11 = jnp.where(allowed, s[half:, half:], LOWEST)
        top0 = jnp.max(s00, axis=0, keepdims=True)
        top1 = jnp.maximum(jnp.max(s01, axis=0, keepdims=True), jnp.max(s11, axis=0, keepdims=True))
        w00 = jnp.exp2((s00 - top0) * (SCALE * LOG2E))
        w01 = jnp.exp2((s01 - top1) * (SCALE * LOG2E))
        w11 = jnp.exp2((s11 - top1) * (SCALE * LOG2E))
        mass0 = jnp.sum(w00, axis=0, keepdims=True)
        mass1 = jnp.sum(w01, axis=0, keepdims=True) + jnp.sum(w11, axis=0, keepdims=True)
        w = jnp.concatenate(
            [
                jnp.concatenate([w00.astype(BF16), w01.astype(BF16)], axis=1),
                jnp.concatenate([jnp.zeros((half, half), BF16), w11.astype(BF16)], axis=1),
            ],
            axis=0,
        )
        o = dot(v_t[HEAD * hh : HEAD * (hh + 1)], w)
        o = o * (1.0 / jnp.concatenate([mass0, mass1], axis=1))
        parts.append(o.astype(BF16))
    turned = jnp.concatenate(parts, axis=0)
    unit = eye(ROWS)
    for j in range(SPAN // LANES):
        cols = pl.ds(pl.multiple_of(group * SPAN + LANES * j, LANES), LANES)
        out[:, cols] = dot(unit, turned[LANES * j : LANES * (j + 1)], NT).astype(BF16)


def local_picks(group, q_pick, k, v, o_pick, lse_pick):
    shape = (GROUP * PICKS, SPAN)
    own = (iota(shape, 0) >> 4) == head_of(iota(shape, 1))
    q = jnp.concatenate([q_pick] * GROUP, axis=0) * jnp.where(own, 1.0, 0.0).astype(BF16)
    s = dot(q, k, NT)
    row, key = iota(s.shape, 0), iota(s.shape, 1)
    residue = ((row >> 4) + group * GROUP) & (COARSE - 1)
    s = jnp.where(key <= (row & (PICKS - 1)) * COARSE + residue, s, LOWEST)
    top = jnp.max(s, axis=1, keepdims=True)
    w = jnp.exp2((s - top) * (SCALE * LOG2E))
    mass = jnp.sum(w, axis=1, keepdims=True)
    o = dot(w.astype(BF16), v) * (1.0 / mass)
    lse = top * SCALE + jnp.log(mass)
    cols = pl.ds(pl.multiple_of(group * SPAN, LANES), SPAN)
    o_pick[:, cols] = jnp.sum(jnp.where(own, o, 0.0).reshape(GROUP, PICKS, SPAN), axis=0)
    lse_pick[:, cols] = jnp.sum(jnp.where(own, lse, 0.0).reshape(GROUP, PICKS, SPAN), axis=0)


def attend(q, parts, lane, turn):
    scores, tops = [], []
    for keys, known in parts:
        if callable(known):
            s = known(dot(q, keys[:, :LANES], NT))
            known = s, jnp.max(s, axis=1, keepdims=True)
        scores.append(known[0])
        tops.append(known[1])
    top = functools.reduce(jnp.maximum, tops)
    weights = [jnp.exp2((s - top) * (SCALE * LOG2E)) for s in scores]
    mass = sum(jnp.sum(w, axis=1, keepdims=True) for w in weights)
    both = sum(dot(w.astype(BF16), keys) for w, (keys, _) in zip(weights, parts))
    o = jnp.where(in_circle(lane, turn + HEAD, 48), both[:, :LANES], pltpu.roll(both[:, LANES:], 48, 1))
    o = o * (1.0 / mass)
    lse = top * SCALE + jnp.log(mass)
    return jnp.where(in_circle(lane, turn + HEAD, HEAD), o, lse)


def place(p, half):
    return (p >> 3) * 16 + half * 8 + (p & 7)


def other_keys(core, other):
    first = other[:, :, :, :, pl.ds(pl.multiple_of(core * 2 * LANES, LANES), LANES)]
    rest = other[:, :, :, :, LANES : 2 * LANES]
    return jnp.concatenate([x.reshape(HALF_ROWS, LANES) for x in (first, rest)], axis=1)


STEP = 128


def near_scores(head, near, scores, tops):
    turn = lax.rem(head * HEAD, LANES)
    own = jnp.where(in_circle(iota((1, LANES), 1), turn, HEAD), 1.0, 0.0).astype(BF16)
    below = iota((STEP, STEP), 1) <= iota((STEP, STEP), 0)
    x = near[...].reshape(HALF_ROWS, 2 * LANES)
    for start in range(0, HALF_ROWS, STEP):
        end = start + STEP
        s = dot(x[start:end, LANES:] * own, x[:end, :LANES], NT)
        last = jnp.where(below, s[:, start:], LOWEST)
        s = last if start == 0 else jnp.concatenate([s[:, :start], last], axis=1)
        scores[start:end, :end] = s
        tops[start:end, :] = jnp.broadcast_to(jnp.max(s, axis=1, keepdims=True), (STEP, LANES))


def coarse_blocks(head, half, near, y, scores, tops, back):
    turn = lax.rem(head * HEAD, LANES)
    own = jnp.where(in_circle(iota((1, LANES), 1), turn, HEAD), 1.0, 0.0).astype(BF16)
    x = near[...].reshape(HALF_ROWS, 2 * LANES)
    for b in range(HALF_ROWS // STEP):
        start, end = b * STEP, (b + 1) * STEP
        parts = [(x[:end], (scores[start:end, :end], tops[start:end, :1]))]
        if b + half > 0:
            parts.append((y[: start + half * STEP], lambda s: s))
        q = x[start:end, LANES:] * own
        back[start:end, :] = attend(q, parts, iota((STEP, LANES), 1), turn)


def far_rows(head, half, grp, x, far):
    turn = lax.rem(head * HEAD, LANES)
    block = 256
    per = block // 8
    chosen = iota((per, block), 1) == iota((per, block), 0) * 8 + head // COARSE
    chosen = jnp.where(chosen, 1.0, 0.0).astype(BF16)
    rows = jnp.concatenate([dot(chosen, x[block * b : block * (b + 1)]) for b in range(HALF_ROWS // block)], axis=0)
    far[grp, half, :FAR] = rows[:, :LANES].astype(BF16)
    rest = rows[:, LANES:]
    packed = rest[:PICKS]
    for i in range(1, FAR // PICKS):
        turned = pltpu.roll(rest[PICKS * i : PICKS * (i + 1)], 32 * i, 1)
        packed = jnp.where(in_circle(iota(packed.shape, 1), turn + HEAD + 32 * i, 32), turned, packed)
    far[grp, half, FAR:] = packed.astype(BF16)
    return rest.astype(BF16)


def far_keys(far):
    count = GRP * 2
    first = far[:, :, :FAR].reshape(count * FAR, LANES)
    packed = far[:, :, FAR:].astype(F32).reshape(count * PICKS, LANES)
    turned = [packed] + [pltpu.roll(packed, LANES - 32 * i, 1) for i in range(1, FAR // PICKS)]
    rest = jnp.stack([x.reshape(count, PICKS, LANES) for x in turned], axis=1).reshape(count * FAR, LANES)
    return jnp.concatenate([first, rest.astype(BF16)], axis=1)


def far_place(r):
    return (r >> 4) * 32 + (r & 15)


def whole_level(head, half, grp, far_q, far, back):
    turn = lax.rem(head * HEAD, LANES)
    own = jnp.where(in_circle(iota((1, LANES), 1), turn, HEAD), 1.0, 0.0).astype(BF16)
    keys = far_keys(far)
    q = far_q[...] * own

    def hide(s):
        row, col = iota(s.shape, 0), iota(s.shape, 1)
        row = grp * (2 * FAR) + half * 16 + far_place(row)
        col = (col >> 7) * (2 * FAR) + ((col >> 6) & 1) * 16 + far_place(col & (FAR - 1))
        return jnp.where(col <= row, s, LOWEST)

    lane = iota((FAR, LANES), 1)
    mine = attend(q, [(keys, hide)], lane, turn)
    rows = pl.ds(head // COARSE, FAR, stride=8)
    other = back[rows, :]
    result = in_circle(lane, turn + HEAD, HEAD)
    l2 = jnp.max(jnp.where(result, LOWEST * 2, other), axis=1, keepdims=True)
    l3 = jnp.max(jnp.where(result, LOWEST * 2, mine), axis=1, keepdims=True)
    best = jnp.maximum(l2, l3)
    e2, e3 = jnp.exp(l2 - best), jnp.exp(l3 - best)
    total = e2 + e3
    back[rows, :] = jnp.where(result, (e2 * other + e3 * mine) / total, best + jnp.log(total))


def merge_group(group, home, o_pick, lse_pick, out):
    lane = iota((PICKS, LANES), 1)
    tiles_o = [jnp.zeros((PICKS, LANES), F32)] * (SPAN // LANES)
    tiles_l = list(tiles_o)
    for hh in range(GROUP):
        tile, shift, tiles = window(hh)
        m = home[group * GROUP + hh]
        o = pltpu.roll(m, 48, 1)
        at = (shift + 40) % LANES
        lse = jnp.broadcast_to(m[:, at : at + 1], (PICKS, LANES))
        for n in range(tiles):
            here = lane >= shift if n == 0 else lane < shift + HEAD - LANES
            tiles_o[tile + n] = jnp.where(here, o, tiles_o[tile + n])
            tiles_l[tile + n] = jnp.where(here, lse, tiles_l[tile + n])
    for n in range(SPAN // LANES):
        cols = pl.ds(pl.multiple_of(group * SPAN + n * LANES, LANES), LANES)
        l1, l2 = lse_pick[:, cols], tiles_l[n]
        best = jnp.maximum(l1, l2)
        e1, e2 = jnp.exp(l1 - best), jnp.exp(l2 - best)
        merged = (e1 * o_pick[:, cols] + e2 * tiles_o[n]) / (e1 + e2)
        shape = (PICKS, COARSE, LANES)
        residue = head_of(iota((1, COARSE, LANES), 2) + (group * SPAN + n * LANES)) & (COARSE - 1)
        chosen = iota((1, COARSE, LANES), 1) == residue
        rows = jnp.where(chosen, merged.reshape(PICKS, 1, LANES), out[:, cols].reshape(shape).astype(F32))
        out[:, cols] = rows.reshape(ROWS, LANES).astype(BF16)


def kernel(
    q_hbm, k_hbm, v_hbm, out,
    q, k, v, q_pick, o_pick, lse_pick, send, send_pair, near, other, far_q, far, scores, tops, back, home,
    in_sem, send_sem, pair_sem, near_sem, other_sem, pass_send, pass_recv, far_send, far_recv, back_send, home_recv,
):
    grp, seq = lax.axis_index("grp"), lax.axis_index("seq")
    half = (seq >> 3) & 1
    head = (seq >> 4) * 8 + (seq & 7)
    core = head & 1
    late = (half == 1) & (head >= HEADS - 8)

    barrier = pltpu.get_barrier_semaphore()

    for h in (1, 0):
        for offset in PLANE:
            for other_core in (1, 0):
                if h or other_core or offset != (0, 0):
                    to = place(beyond(head, offset) ^ other_core, half ^ h)
                    pl.semaphore_signal(barrier, inc=1, device_id=(grp, to), device_id_type=MESH)
        for d in range(1, GRP):
            pl.semaphore_signal(barrier, inc=1, device_id=(grp ^ d, seq ^ (8 * h)), device_id_type=MESH)

    def load(group, n):
        cols = pl.ds(pl.multiple_of(group * SPAN, LANES), SPAN)
        x, y = ((q_hbm, q), (k_hbm, k), (v_hbm, v))[n]
        return pltpu.make_async_copy(x.at[:, cols], y.at[:, cols], in_sem.at[group, n])

    for group in range(GROUPS):
        load(group, 1).start()
        load(group, 2).start()
    for group in range(GROUPS):
        load(group, 0).start()

    gather = jnp.where((iota((PICKS, ROWS), 1) >> 4) == iota((PICKS, ROWS), 0), 1.0, 0.0).astype(BF16)

    def pack(group, _):
        load(group, 1).wait()
        load(group, 2).wait()
        cols = pl.ds(pl.multiple_of(group * SPAN, LANES), SPAN)
        pack_keys(group, k[:, cols], v[:, cols], group_mask(group), gather, send, send_pair)
        return 0

    def pack_rest(group, _):
        load(group, 0).wait()
        cols = pl.ds(pl.multiple_of(group * SPAN, LANES), SPAN)
        pack_queries(group, q[:, cols], group_mask(group), gather, send, q_pick)
        return 0

    lax.fori_loop(0, GROUPS, pack, 0)

    def local(group, _):
        cols = pl.ds(pl.multiple_of(group * SPAN, LANES), SPAN)
        local_picks(group, q_pick[group], k[:, cols], v[:, cols], o_pick, lse_pick)
        local_group(group, q[:, cols], k[:, cols], v[:, cols], out)
        return 0

    ahead = jnp.where(half == 0, 2, 0)

    @pl.when(half == 0)
    def _():
        lax.fori_loop(0, GROUPS, pack_rest, 0)
        lax.fori_loop(0, ahead, local, 0)

    pl.semaphore_wait(barrier, SEQ - 1 + 2 * (GRP - 1))

    yields = (half == 1) & (grp == GRP - 1)

    def across(offsets):
        for offset in offsets:
            to = beyond(head, offset)
            pltpu.make_async_remote_copy(
                src_ref=send_pair.at[to >> 1], dst_ref=other.at[head >> 3, core, (head >> 1) & 3],
                send_sem=pair_sem, recv_sem=other_sem.at[head >> 3],
                device_id=(grp, place(to, 1 - half)), device_id_type=MESH,
            ).start()

    splits = (half == 1) & (grp == 0)

    @pl.when(jnp.logical_not(late | yields))
    def _():
        across(PLANE[:8])

    @pl.when(jnp.logical_not(late | yields | splits))
    def _():
        across(PLANE[8:])

    @pl.when(half == 1)
    def _():
        lax.fori_loop(0, GROUPS, pack_rest, 0)

    for offset in PLANE:
        for other_core in (1, 0):
            if other_core or offset != (0, 0):
                to = beyond(head, offset) ^ other_core
                pltpu.make_async_remote_copy(
                    src_ref=send.at[to], dst_ref=near.at[head], send_sem=send_sem, recv_sem=near_sem,
                    device_id=(grp, place(to, half)), device_id_type=MESH,
                ).start()
    pltpu.make_async_copy(send.at[head], near.at[head], near_sem).start()

    @pl.when(jnp.logical_not(late) & yields)
    def _():
        across(PLANE[:8])

    @pl.when(jnp.logical_not(late) & (yields | splits))
    def _():
        across(PLANE[8:])

    lax.fori_loop(ahead, jnp.maximum(ahead, 1), local, 0)

    for g in range(1, GRP):
        @pl.when(grp < g)
        def _():
            far[g] = jnp.zeros((2, FAR + PICKS, LANES), BF16)

    @pl.when(half == 0)
    def _():
        other[3] = jnp.zeros((2, 4, PICKS, 3 * LANES), BF16)

    pltpu.make_async_copy(near, near, near_sem).wait()
    far_q[...] = far_rows(head, half, grp, near[...].reshape(HALF_ROWS, 2 * LANES), far)

    def far_copy(to, h):
        return pltpu.make_async_remote_copy(
            src_ref=far.at[grp, half], dst_ref=far.at[grp, half],
            send_sem=far_send.at[to, h], recv_sem=far_recv.at[grp, half],
            device_id=(to, place(head, h)), device_id_type=MESH,
        )

    for to in range(1, GRP):
        @pl.when(to > grp)
        def _():
            far_copy(to, half).start()
            far_copy(to, 1 - half).start()

    near_scores(head, near, scores, tops)
    lax.fori_loop(jnp.maximum(ahead, 1), jnp.maximum(ahead, 2), local, 0)

    def pass_on(x):
        part = other.at[x, core, :, :, pl.ds(pl.multiple_of((1 - core) * LANES, LANES), 2 * LANES)]
        return pltpu.make_async_remote_copy(
            src_ref=part, dst_ref=part, send_sem=pass_send.at[x], recv_sem=pass_recv.at[x],
            device_id=(grp, seq ^ 1), device_id_type=MESH,
        )

    for part in range(2):
        @pl.when(half == part)
        def _():
            for x in range(3 + part):
                here = other.at[x, core]
                pltpu.make_async_copy(here, here, other_sem.at[x]).wait()
                pass_on(x).start()
            for x in range(3 + part):
                pass_on(x).wait()
            y = other_keys(core, other)
            far_rows(head, 1 - part, grp, y, far)
            coarse_blocks(head, part, near, y, scores, tops, back)

    for g in range(GRP - 1):
        @pl.when(grp > g)
        def _():
            for h in range(2):
                pltpu.make_async_copy(far.at[g, h], far.at[g, h], far_recv.at[g, h]).wait()

    whole_level(head, half, grp, far_q, far, back)

    for offset in PLANE:
        for other_core in (1, 0):
            if other_core or offset != (0, 0):
                to = beyond(head, offset) ^ other_core
                rows = pl.ds(pl.multiple_of(to * PICKS, PICKS), PICKS)
                pltpu.make_async_remote_copy(
                    src_ref=back.at[rows], dst_ref=home.at[head],
                    send_sem=back_send, recv_sem=home_recv.at[head // GROUP],
                    device_id=(grp, place(to, half)), device_id_type=MESH,
                ).start()
    rows = pl.ds(pl.multiple_of(head * PICKS, PICKS), PICKS)
    pltpu.make_async_copy(back.at[rows], home.at[head], home_recv.at[head // GROUP]).start()

    lax.fori_loop(jnp.maximum(ahead, 2), GROUPS, local, 0)

    def merge(group, _):
        part = home.at[pl.ds(group * GROUP, GROUP)]
        pltpu.make_async_copy(part, part, home_recv.at[group]).wait()
        merge_group(group, home, o_pick, lse_pick, out)
        return 0

    lax.fori_loop(0, GROUPS, merge, 0)

    most = send.at[pl.ds(0, HEADS - 1)]
    pltpu.make_async_copy(most, most, send_sem).wait()

    @pl.when(jnp.logical_not(late))
    def _():
        pltpu.make_async_copy(send_pair, send_pair, pair_sem).wait()

    for to in range(1, GRP):
        @pl.when(to > grp)
        def _():
            for h in range(2):
                pltpu.make_async_copy(far.at[0, 0], far.at[0, 0], far_send.at[to, h]).wait()
    most = back.at[pl.ds(0, (HEADS - 1) * PICKS)]
    pltpu.make_async_copy(most, most, back_send).wait()


def body(queries, key_matrix, value_matrix):
    return pl.pallas_call(
        kernel,
        out_shape=jax.ShapeDtypeStruct((ROWS, WIDTH), BF16),
        in_specs=[pl.BlockSpec(memory_space=pltpu.HBM)] * 3,
        out_specs=pl.BlockSpec(memory_space=pltpu.VMEM),
        scratch_shapes=[
            pltpu.VMEM((ROWS, WIDTH), BF16),
            pltpu.VMEM((ROWS, WIDTH), BF16),
            pltpu.VMEM((ROWS, WIDTH), BF16),
            pltpu.VMEM((GROUPS, PICKS, SPAN), BF16),
            pltpu.VMEM((PICKS, WIDTH), F32),
            pltpu.VMEM((PICKS, WIDTH), F32),
            pltpu.VMEM((HEADS, PICKS, 2 * LANES), BF16),
            pltpu.VMEM((HEADS // 2, PICKS, 3 * LANES), BF16),
            pltpu.VMEM((HEADS, PICKS, 2 * LANES), BF16),
            pltpu.VMEM((4, 2, 4, PICKS, 3 * LANES), BF16),
            pltpu.VMEM((FAR, LANES), BF16),
            pltpu.VMEM((GRP, 2, FAR + PICKS, LANES), BF16),
            pltpu.VMEM((HALF_ROWS, HALF_ROWS), F32),
            pltpu.VMEM((HALF_ROWS, LANES), F32),
            pltpu.VMEM((HALF_ROWS, LANES), F32),
            pltpu.VMEM((HEADS, PICKS, LANES), F32),
            pltpu.SemaphoreType.DMA((GROUPS, 3)),
            pltpu.SemaphoreType.DMA,
            pltpu.SemaphoreType.DMA,
            pltpu.SemaphoreType.DMA,
            pltpu.SemaphoreType.DMA((4,)),
            pltpu.SemaphoreType.DMA((4,)),
            pltpu.SemaphoreType.DMA((4,)),
            pltpu.SemaphoreType.DMA((GRP, 2)),
            pltpu.SemaphoreType.DMA((GRP, 2)),
            pltpu.SemaphoreType.DMA,
            pltpu.SemaphoreType.DMA((GROUPS,)),
        ],
        compiler_params=pltpu.CompilerParams(
            collective_id=0, has_side_effects=True, vmem_limit_bytes=48 * 1024 * 1024
        ),
    )(*(pltpu.with_memory_space_constraint(x, pltpu.HBM) for x in (queries, key_matrix, value_matrix)))


def solution(mesh):
    placed = P(("grp", "seq"), None)
    return jax.shard_map(
        body, mesh=mesh, in_specs=(placed,) * 3, out_specs=placed, check_vma=False
    )
```
